256 devices in a mesh: ctx: 16 (over x, y), vis: 16 (over z, core).
Axes of the slice: x: 4, y: 4, z: 8, core: 2. Of those that a mesh axis runs over, the one named last changes fastest.
Arguments:
- patches: bfloat16 [32768, 1280], P(('ctx', 'vis')), may hold values from -10 to 10
- vis_gain: float32 [1280], replicated, may hold values from 0.5 to 1.5
- w_qkv: bfloat16 [1280, 3840], P(None, 'vis'), may hold values from -2 to 2
- w_out: bfloat16 [1280, 1280], P('vis'), may hold values from -0.15625 to 0.15625
- merge_gain: float32 [1280], replicated, may hold values from 0.5 to 1.5
- w_merge: bfloat16 [5120, 8192], P(None, 'vis'), may hold values from -0.078125 to 0.078125
- token_dest: int32 [16, 512], replicated, may hold values from 0 to 15, as said below
- token_row: int32 [16, 512], replicated, may hold values from 0 to 1023, as said below
- prompt_text: bfloat16 [16384, 8192], P('ctx', 'vis'), may hold values from -6 to 6
- kv_gain: float32 [8192], P('vis'), may hold values from 0.5 to 1.5
- w_kv: bfloat16 [8192, 1024], P('vis'), may hold values from -1 to 1
- queries: bfloat16 [2048, 4096], P('ctx'), may hold values from -12 to 12
- resp_kv: bfloat16 [2048, 1024], P('ctx'), may hold values from -12 to 12
- resp_len: int32 [16], P('ctx'), may hold values from 64 to 128
Outputs:
- attended: bfloat16 [2048, 4096], P('ctx')
The draws below stay inside these ranges and needn't reach their ends.
Inputs may be any that keep to these rules, and one draw needn't show every extreme that they name: `token_dest`: the tokens of one image are in order of their prompt shard; at most 48 tokens of one image go to one shard, and from every image exactly 48 go to some shard. `token_row`: no two visual tokens take the same position of one shard.
All inputs are finite; a program needn't handle non-finite values.
Results may differ from the reference program's by a relative error of at most 0.014.
Values may be sent and summed in bfloat16 or wider, within the bound.
No kernel may reach another device: no remote copies, remote signals or barrier semaphores. Data moves between devices by JAX's collectives and lax.ppermute only.
A program may use at most 128 MiB of HBM per device.

```python
import math
import jax
import jax.numpy as jnp
from jax import lax

VD = 1280
VHEADS = 16
D = 8192
HD = 128
QH = 32
KVH = 4
CROWS = 1024
R_TOK = 128
VHD = 80
MD = 5120
GP = 2048
VTOK = 512
IMAGES = 16
BASE = 32
L = 16384
RESP = 2048
N_CTX = 16


def routing_tables(key):
    count = IMAGES
    half = BASE // 2
    spare = jax.random.randint(jax.random.fold_in(key, 11), (count, count), 0, half + 1)
    diagonal = jnp.arange(count)
    spare = spare.at[diagonal, diagonal].set(half)
    spare = spare.at[diagonal, (diagonal + 1) % count].set(0)
    amounts = BASE + spare - jnp.roll(spare, -1, axis=1)
    running = jnp.cumsum(amounts, axis=1)
    tokens = jnp.arange(VTOK)
    dest = jnp.sum((tokens[None, :, None] >= running[:, None, :]).astype(jnp.int32), axis=2)
    row_first = running - amounts
    within = tokens[None, :] - jnp.take_along_axis(row_first, dest, axis=1)
    column_first = jnp.cumsum(amounts, axis=0) - amounts
    offset = jnp.take_along_axis(column_first, dest, axis=1)
    keys = jax.random.split(jax.random.fold_in(key, 12), count)
    orders = jax.vmap(lambda single: jax.random.permutation(single, CROWS))(keys)
    rows = orders[dest, offset + within]
    return (dest.astype(jnp.int32), rows.astype(jnp.int32))


def draw_token_dest(key, part):
    return routing_tables(key)[0]


def draw_token_row(key, part):
    return routing_tables(key)[1]


def draw_patches(key, part):
    shape = (N_CTX * GP, VD)
    noise_key = jax.random.fold_in(key, 41)
    base = jax.random.truncated_normal(noise_key, -6.0, 6.0, shape, jnp.float32)
    return base.astype(jnp.bfloat16)


def draw_w_qkv(key, part):
    base = jax.random.truncated_normal(jax.random.fold_in(key, 51), -6.0, 6.0, (VD, 3 * VD), jnp.float32)
    base = base / math.sqrt(VD)
    return base.astype(jnp.bfloat16)


def draw_prompt_text(key, part):
    shape = (L, D)
    noise_key = jax.random.fold_in(key, 81)
    base = jax.random.truncated_normal(noise_key, -6.0, 6.0, shape, jnp.float32)
    return base.astype(jnp.bfloat16)


def draw_w_kv(key, part):
    width = KVH * HD
    base = jax.random.truncated_normal(jax.random.fold_in(key, 91), -6.0, 6.0, (D, 2 * width), jnp.float32)
    base = base / math.sqrt(D)
    return base.astype(jnp.bfloat16)


def draw_resp_kv(key, part):
    shape = (RESP, 2 * KVH * HD)
    noise_key = jax.random.fold_in(key, 61)
    base = jax.random.truncated_normal(noise_key, -6.0, 6.0, shape, jnp.float32)
    return base.astype(jnp.bfloat16)


def draw_queries(key, part):
    shape = (RESP, QH * HD)
    noise_key = jax.random.fold_in(key, 71)
    base = 3.0 * jax.random.truncated_normal(noise_key, -4.0, 4.0, shape, jnp.float32)
    return base.astype(jnp.bfloat16)


def set_ends(values, own_key, smallest, high):
    shape = values.shape
    place = [jax.random.randint(jax.random.fold_in(own_key, axis), (), 0, shape[axis]) for axis in range(len(shape))]
    values = values.at[tuple(place)].set(smallest)
    longest = shape.index(max(shape))
    place[longest] = (place[longest] + 1) % shape[longest]
    return values.at[tuple(place)].set(high)


def block_scale(stream_key, extent, cuts, smallest, largest):
    loudness, own = 1.0, jax.random.fold_in(stream_key, 6)
    for dim, shards_of in cuts:
        heights = jnp.exp(jax.random.uniform(jax.random.fold_in(own, dim), (shards_of,), jnp.float32, smallest / len(cuts), largest / len(cuts)))
        loudness = loudness * jnp.repeat(heights, extent[dim] // shards_of).reshape([-1 if axis == dim else 1 for axis in range(len(extent))])
    return loudness


def bell_draw(rng, dims, deviation, bound, cuts=(), held_as=jnp.bfloat16):
    entries = jax.random.normal(rng, dims, jnp.float32) * deviation
    if len(cuts) > 0:
        entries = block_scale(rng, dims, cuts, -0.22, 0.18) * entries
    return jnp.clip(entries, min=-bound, max=bound).astype(held_as)


def setup_inputs(seed: int = 0) -> dict:
    key_list = jax.random.split(jax.random.key(seed), 15)
    patches = draw_patches(jax.random.fold_in(key_list[14], 71), 0)
    vis_gain = jnp.clip(1.0 + 0.1 * jax.random.normal(key_list[1], (VD,), jnp.float32), 0.5, 1.5)
    w_qkv = draw_w_qkv(jax.random.fold_in(key_list[14], 71), 0)
    w_out = bell_draw(key_list[3], (VD, VD), VD ** -0.5, 0.15625, ((0, 16),))
    merge_gain = jnp.clip(1.0 + 0.1 * jax.random.normal(key_list[4], (VD,), jnp.float32), 0.5, 1.5)
    w_merge = bell_draw(key_list[5], (MD, D), MD ** -0.5, 0.078125, ((1, 16),))
    token_dest = draw_token_dest(jax.random.fold_in(key_list[14], 71), 0)
    token_row = draw_token_row(jax.random.fold_in(key_list[14], 71), 0)
    prompt_text = draw_prompt_text(jax.random.fold_in(key_list[14], 71), 0)
    kv_gain = jnp.clip(1.0 + 0.1 * jax.random.normal(key_list[9], (D,), jnp.float32), 0.5, 1.5)
    w_kv = draw_w_kv(jax.random.fold_in(key_list[14], 71), 0)
    queries = draw_queries(jax.random.fold_in(key_list[14], 71), 0)
    resp_kv = draw_resp_kv(jax.random.fold_in(key_list[14], 71), 0)
    resp_len = set_ends(jax.random.randint(key_list[13], (N_CTX,), R_TOK // 2, R_TOK + 1), jax.random.fold_in(key_list[13], 1), R_TOK // 2, R_TOK).astype(jnp.int32)
    return {"patches": patches, "vis_gain": vis_gain, "w_qkv": w_qkv, "w_out": w_out, "merge_gain": merge_gain, "w_merge": w_merge, "token_dest": token_dest, "token_row": token_row, "prompt_text": prompt_text, "kv_gain": kv_gain, "w_kv": w_kv, "queries": queries, "resp_kv": resp_kv, "resp_len": resp_len}


EPS = 1e-06

def layer_norm(values, gain):
    center = values - lax.optimization_barrier(jnp.mean(values, axis=-1, keepdims=True))
    spread = lax.optimization_barrier(jnp.mean(center * center, axis=-1, keepdims=True))
    return center * lax.rsqrt(spread + EPS) * gain.astype(jnp.float32)

def dense_attention(query, keys, values):
    count = query.shape[0]
    block = min(512, count)
    scale = 1.0 / math.sqrt(query.shape[1])

    def one_block(part):
        scores = jnp.dot(part, keys.T, preferred_element_type=jnp.float32) * scale
        highest = lax.optimization_barrier(jnp.max(scores, axis=1, keepdims=True))
        expo = jnp.exp(scores - highest)
        summed = lax.optimization_barrier(jnp.sum(expo, axis=1, keepdims=True))
        mixed = jnp.dot(expo.astype(jnp.bfloat16), values, preferred_element_type=jnp.float32)
        return (mixed / summed).astype(jnp.bfloat16)
    blocks = query.reshape(count // block, block, query.shape[1])
    return lax.map(one_block, blocks).reshape(count, values.shape[1])

def head_attention(packed):
    stacked = jnp.transpose(packed, (1, 0, 2))

    def one_head(item):
        return dense_attention(item[:, :VHD], item[:, VHD:2 * VHD], item[:, 2 * VHD:])
    return jnp.transpose(lax.map(one_head, stacked), (1, 0, 2))

def reference(patches, vis_gain, w_qkv, w_out, merge_gain, w_merge, token_dest, token_row, prompt_text, kv_gain, w_kv, queries, resp_kv, resp_len):

    def vision_image(patch_rows):
        floats = patch_rows.astype(jnp.float32)
        normed = layer_norm(floats, vis_gain).astype(jnp.bfloat16)
        qkv = jnp.dot(normed, w_qkv, preferred_element_type=jnp.float32).astype(jnp.bfloat16)
        heads = head_attention(qkv.reshape(GP, VHEADS, 3 * VHD)).reshape(GP, VD)
        mixed = floats + jnp.dot(heads, w_out, preferred_element_type=jnp.float32)
        merged = layer_norm(mixed, merge_gain).astype(jnp.bfloat16).reshape(VTOK, MD)
        return jnp.dot(merged, w_merge, preferred_element_type=jnp.float32).astype(jnp.bfloat16)
    visual = lax.map(vision_image, patches.reshape(IMAGES, GP, VD))
    places = (token_dest * CROWS + token_row).reshape(-1).astype(jnp.int32)
    prompt = prompt_text.at[places].set(visual.reshape(IMAGES * VTOK, D))

    def project_block(rows):
        floats = rows.astype(jnp.float32)
        inverse = lax.rsqrt(lax.optimization_barrier(jnp.mean(floats * floats, axis=1, keepdims=True)) + EPS)
        normed = (floats * inverse * kv_gain.astype(jnp.float32)).astype(jnp.bfloat16)
        return jnp.dot(normed, w_kv, preferred_element_type=jnp.float32).astype(jnp.bfloat16)
    kv = lax.map(project_block, prompt.reshape(N_CTX, CROWS, D)).reshape(L, 2 * KVH * HD)
    width = KVH * HD
    prompt_keys = kv[:, :width].reshape(L, KVH, HD)
    prompt_values = kv[:, width:].reshape(L, KVH, HD)
    group = QH // KVH
    scale = 1.0 / math.sqrt(HD)
    position = jnp.arange(R_TOK, dtype=jnp.int32)
    visible = jnp.concatenate([jnp.ones((R_TOK, L), dtype=bool), position[None, :] <= position[:, None]], axis=1)

    def one_response(items):
        query, own, length = items
        q_heads = jnp.transpose(query.reshape(R_TOK, KVH, group, HD), (1, 0, 2, 3))
        keys = jnp.concatenate([prompt_keys, own[:, :width].reshape(R_TOK, KVH, HD)], axis=0)
        values = jnp.concatenate([prompt_values, own[:, width:].reshape(R_TOK, KVH, HD)], axis=0)
        keys = jnp.transpose(keys, (1, 0, 2))
        values = jnp.transpose(values, (1, 0, 2))

        def one_head(triple):
            q_part, k_part, v_part = triple
            scores = jnp.einsum('rgd,nd->grn', q_part.astype(jnp.float32), k_part.astype(jnp.float32)) * scale
            scores = jnp.where(visible[None], scores, -1e+30)
            highest = lax.optimization_barrier(jnp.max(scores, axis=2, keepdims=True))
            expo = jnp.where(visible[None], jnp.exp(scores - highest), 0.0)
            summed = lax.optimization_barrier(jnp.sum(expo, axis=2, keepdims=True))
            mixed = jnp.einsum('grn,nd->grd', expo.astype(jnp.bfloat16).astype(jnp.float32), v_part.astype(jnp.float32))
            return mixed / summed
        result = lax.map(one_head, (q_heads, keys, values))
        result = jnp.transpose(result, (2, 0, 1, 3)).reshape(R_TOK, QH * HD)
        live = (position < length)[:, None]
        return jnp.where(live, result, 0.0).astype(jnp.bfloat16)
    attended = lax.map(one_response, (queries.reshape(N_CTX, R_TOK, QH * HD), resp_kv.reshape(N_CTX, R_TOK, 2 * width), resp_len))
    return attended.reshape(RESP, QH * HD)
```

```python
import math

import jax
import jax.numpy as jnp
from jax import lax
from jax.experimental import pallas as pl
from jax.experimental.pallas import tpu as pltpu
from jax.sharding import PartitionSpec as P

VD = 1280
VHEADS = 16
D = 8192
HD = 128
QH = 32
KVH = 4
CROWS = 1024
R_TOK = 128
VHD = 80
GP = 2048
VTOK = 512
N = 16
LOCAL = GP // N
EPS = 1e-06
NEG = -1e30
bf16 = jnp.bfloat16
f32 = jnp.float32

SWAP = [(i, i ^ 1) for i in range(N)]
QUADS = [[4 * g + i for i in range(4)] for g in range(4)]
RING_ORDER = (0, 1, 2, 3, -1, -2, -3, 4)


def along_z(shift):
    return [(z * 2 + c, ((z + shift) % 8) * 2 + c) for z in range(8) for c in range(2)]


def ring_gather(block):
    ups = [block]
    downs = [block]
    for step in range(1, 4):
        ups.append(lax.ppermute(ups[-1], "vis", along_z(1)))
        downs.append(lax.ppermute(downs[-1], "vis", along_z(-1)))
    half = block.shape[0] // 2
    up = lax.ppermute(ups[-1][:half], "vis", along_z(1))
    down = lax.ppermute(downs[-1][half:], "vis", along_z(-1))
    mine = jnp.concatenate(ups + downs[1:] + [up, down], axis=0)
    return jnp.concatenate([mine, lax.ppermute(mine, "vis", SWAP)], axis=0)


def ring_owners(vis_index):
    z = vis_index // 2
    core = vis_index % 2
    zs = (z - jnp.array(RING_ORDER, jnp.int32)) % 8
    return jnp.concatenate([zs * 2 + core, zs * 2 + 1 - core])


def dot(a, b, contract):
    return lax.dot_general(a, b, ((contract[:1], contract[1:]), ((), ())), preferred_element_type=f32)


def normed_rows(values, gain):
    center = values - jnp.mean(values, axis=-1, keepdims=True)
    spread = jnp.mean(center * center, axis=-1, keepdims=True)
    return center * lax.rsqrt(spread + EPS) * gain


QKV_STEPS = 4
QKV_ROWS = GP // QKV_STEPS
ATT_STEPS = 8
ATT_ROWS = GP // ATT_STEPS


def vision_kernel(x_ref, gain_ref, w_ref, out_ref, q_s, k_s, v_s):
    step = pl.program_id(0)

    @pl.when(step < QKV_STEPS)
    def _():
        normed = normed_rows(x_ref[...].astype(f32), gain_ref[...]).astype(bf16)
        qkv = dot(normed, w_ref[...], (1, 0)).astype(bf16)
        rows = pl.ds(pl.multiple_of(step * QKV_ROWS, QKV_ROWS), QKV_ROWS)
        q_s[rows, :] = qkv[:, :128]
        k_s[rows, :] = qkv[:, 128:256]
        v_s[rows, :] = qkv[:, 256:]

    @pl.when(step >= QKV_STEPS)
    def _():
        first = pl.multiple_of((step - QKV_STEPS) * ATT_ROWS, ATT_ROWS)
        query = q_s[pl.ds(first, ATT_ROWS), :]
        scores = dot(query, k_s[...], (1, 1)) * (1.0 / math.sqrt(VHD))
        highest = jnp.max(scores, axis=1, keepdims=True)
        expo = jnp.exp(scores - highest)
        total = jnp.sum(expo, axis=1, keepdims=True)
        mixed = dot(expo.astype(bf16), v_s[...], (1, 0)) / total
        out_ref[...] = jnp.transpose(mixed, (1, 0))[:VHD, :].astype(bf16)


def vision(x, gain, w):
    return pl.pallas_call(
        vision_kernel,
        grid=(QKV_STEPS + ATT_STEPS,),
        in_specs=[
            pl.BlockSpec((QKV_ROWS, VD), lambda i: (jnp.minimum(i, QKV_STEPS - 1), 0)),
            pl.BlockSpec((1, VD), lambda i: (0, 0)),
            pl.BlockSpec((VD, 384), lambda i: (0, 0)),
        ],
        out_specs=pl.BlockSpec((VHD, ATT_ROWS), lambda i: (0, jnp.maximum(i - QKV_STEPS, 0))),
        out_shape=jax.ShapeDtypeStruct((VHD, GP), bf16),
        scratch_shapes=[pltpu.VMEM((GP, 128), bf16)] * 3,
        compiler_params=pltpu.CompilerParams(vmem_limit_bytes=40 * 2**20),
        name="vision",
    )(x, gain, w)


MERGE_STEPS = 4
MERGE_ROWS = GP // MERGE_STEPS
MERGE_TOK = VTOK // MERGE_STEPS
CHUNK = 72


def merge_kernel(order_ref, h_ref, x_ref, wo_ref, gain_ref, wm_ref, kg_ref, wk_ref, out_ref, wo_s):
    @pl.when(pl.program_id(0) == 0)
    def _():
        for k in range(N):
            wo_s[VHD * k : VHD * k + VHD, :] = wo_ref[order_ref[k]]

    mixed = x_ref[...].astype(f32) + dot(h_ref[...], wo_s[...], (0, 0))
    merged = normed_rows(mixed, gain_ref[...]).astype(bf16)
    pieces = merged.reshape(MERGE_ROWS // LOCAL, 4, LOCAL // 4, VD)
    visual = dot(pieces[:, 0].reshape(MERGE_TOK, VD), wm_ref[:VD, :], (1, 0))
    for a in range(1, 4):
        part = pieces[:, a].reshape(MERGE_TOK, VD)
        visual += dot(part, wm_ref[a * VD : (a + 1) * VD, :], (1, 0))
    visual = visual.astype(bf16).astype(f32)
    squares = jnp.sum(visual * visual, axis=1, keepdims=True)
    eye = lax.broadcasted_iota(jnp.int32, (MERGE_TOK, MERGE_TOK), 0) == lax.broadcasted_iota(
        jnp.int32, (MERGE_TOK, MERGE_TOK), 1
    )
    row = jnp.sum(jnp.where(eye, squares, 0.0), axis=0, keepdims=True)
    high = row.astype(bf16).astype(f32)
    middle = (row - high).astype(bf16).astype(f32)
    low = row - high - middle
    extra = jnp.concatenate([high, middle, low, jnp.zeros((5, MERGE_TOK), f32)], axis=0)
    gained = (visual * kg_ref[...]).astype(bf16)
    kv = dot(wk_ref[...], gained, (0, 1))
    for v in range(N):
        both = jnp.concatenate([kv[64 * v : 64 * v + 64, :], extra], axis=0)
        out_ref[v, :, :] = both.astype(bf16)


def merge(order, heads, x, w_out, gain, w_merge, kv_gain, w_kv):
    whole = lambda i, order: (0, 0)
    grid_spec = pltpu.PrefetchScalarGridSpec(
        num_scalar_prefetch=1,
        grid=(MERGE_STEPS,),
        in_specs=[
            pl.BlockSpec((VD, MERGE_ROWS), lambda i, order: (0, i)),
            pl.BlockSpec((MERGE_ROWS, VD), lambda i, order: (i, 0)),
            pl.BlockSpec((N, VHD, VD), lambda i, order: (0, 0, 0)),
            pl.BlockSpec((1, VD), whole),
            pl.BlockSpec((4 * VD, 512), whole),
            pl.BlockSpec((1, 512), whole),
            pl.BlockSpec((512, 1024), whole),
        ],
        out_specs=pl.BlockSpec((N, CHUNK, MERGE_TOK), lambda i, order: (0, 0, i)),
        scratch_shapes=[pltpu.VMEM((VD, VD), bf16)],
    )
    return pl.pallas_call(
        merge_kernel,
        grid_spec=grid_spec,
        out_shape=jax.ShapeDtypeStruct((N, CHUNK, VTOK), bf16),
        compiler_params=pltpu.CompilerParams(vmem_limit_bytes=56 * 2**20),
        name="merge",
    )(order, heads, x, w_out, gain, w_merge, kv_gain, w_kv)


PACK = 272


def response_kernel(qa_ref, qb_ref, text_ref, mask_ref, vis_ref, out_ref):
    qa = qa_ref[0]
    qb = qb_ref[0]
    query = jnp.concatenate([qa[:, :HD], qb[:, :HD], qa[:, HD:], qb[:, HD:]], axis=0)
    scale = 1.0 / math.sqrt(HD)
    first = dot(query, text_ref[:HD, :], (1, 0)) * scale + mask_ref[...]
    second = dot(query, vis_ref[:HD, :], (1, 0)) * scale
    highest = jnp.maximum(
        jnp.max(first, axis=1, keepdims=True), jnp.max(second, axis=1, keepdims=True)
    )
    first = jnp.exp(first - highest)
    second = jnp.exp(second - highest)
    total = jnp.sum(first, axis=1, keepdims=True) + jnp.sum(second, axis=1, keepdims=True)
    mixed = dot(first.astype(bf16), text_ref[HD:, :], (1, 1)) + dot(
        second.astype(bf16), vis_ref[HD:, :], (1, 1)
    )
    out_ref[0, : 2 * R_TOK, :] = (mixed / total).astype(bf16)
    level = highest + jnp.log(total)
    eye = lax.broadcasted_iota(jnp.int32, (256, 256), 0) == lax.broadcasted_iota(
        jnp.int32, (256, 256), 1
    )
    row = jnp.sum(jnp.where(eye, level, 0.0), axis=0, keepdims=True)
    high = row.astype(bf16).astype(f32)
    middle = (row - high).astype(bf16).astype(f32)
    low = row - high - middle
    parts = [part[:, k * 128 : k * 128 + 128] for part in (high, middle, low) for k in range(2)]
    tail = jnp.concatenate(parts + [jnp.zeros((10, 128), f32)], axis=0)
    out_ref[0, 2 * R_TOK :, :] = tail.astype(bf16)


def response(qa, qb, text, mask, vis):
    whole = lambda i: (0, 0)
    return pl.pallas_call(
        response_kernel,
        grid=(N,),
        in_specs=[
            pl.BlockSpec((1, R_TOK // 2, 2 * HD), lambda i: (i, 0, 0)),
            pl.BlockSpec((1, R_TOK // 2, 2 * HD), lambda i: (i, 0, 0)),
            pl.BlockSpec((2 * HD, CROWS), whole),
            pl.BlockSpec((1, CROWS), whole),
            pl.BlockSpec((2 * HD, VTOK), whole),
        ],
        out_specs=pl.BlockSpec((1, PACK, HD), lambda i: (i, 0, 0)),
        out_shape=jax.ShapeDtypeStruct((N, PACK, HD), bf16),
        compiler_params=pltpu.CompilerParams(vmem_limit_bytes=40 * 2**20),
        name="response",
    )(qa, qb, text, mask, vis)


def per_device(
    patches,
    vis_gain,
    w_qkv,
    w_out,
    merge_gain,
    w_merge,
    token_dest,
    token_row,
    prompt_text,
    kv_gain,
    w_kv,
    queries,
    resp_kv,
    resp_len,
):
    ctx_index = lax.axis_index("ctx")
    vis_index = lax.axis_index("vis")
    group = vis_index // 4

    local = patches.reshape(LOCAL // 4, 4, VD).transpose(1, 0, 2).reshape(LOCAL, VD)
    image = lax.all_gather(local, "vis", axis=0, tiled=True)

    own_q = lax.dynamic_slice_in_dim(queries, vis_index * 256, 256, 1)
    half = R_TOK // 2
    qa = lax.all_gather(own_q[:half], "ctx", axis=0)
    qb = lax.all_gather(own_q[half:], "ctx", axis=0)

    w_kv_mine = w_kv.reshape(512, 2, KVH, 2, 64).transpose(0, 2, 1, 3, 4).reshape(512, 1024)
    text = prompt_text.astype(f32)
    text_squares = jnp.sum(text * text, axis=1)
    text_gained = (text * kv_gain).astype(bf16)
    text_part = dot(w_kv_mine, text_gained, (0, 1)).reshape(N, 64, CROWS)
    text_extra = jnp.broadcast_to(text_squares[None, None, :], (N, 8, CROWS))
    text_part = jnp.concatenate([text_part, text_extra], axis=1).reshape(N * CHUNK, CROWS)

    flat_dest = token_dest.reshape(-1)
    flat_row = token_row.reshape(-1)
    here = jnp.where(flat_dest == ctx_index, flat_row // 128, -1)
    tall = (here[None, :] == jnp.arange(8, dtype=jnp.int32)[:, None]).astype(bf16)
    wide = ((flat_row % 128)[:, None] == jnp.arange(128, dtype=jnp.int32)[None, :]).astype(bf16)
    taken = dot(tall, wide, (1, 0)).reshape(1, CROWS)
    mask = jnp.where(taken > 0.5, NEG, 0.0)

    own_k = lax.dynamic_slice_in_dim(resp_kv, group * HD, HD, 1)
    own_v = lax.dynamic_slice_in_dim(resp_kv, KVH * HD + group * HD, HD, 1)
    positions = jnp.arange(R_TOK, dtype=jnp.int32)
    visible = positions[None, :] <= positions[:, None]
    q_two = own_q.reshape(R_TOK, 2, HD)
    own_scores = jnp.einsum("rhd,nd->hrn", q_two, own_k, preferred_element_type=f32)
    own_scores = jnp.where(visible, own_scores * (1.0 / math.sqrt(HD)), NEG)
    own_high = jnp.max(own_scores, axis=2, keepdims=True)
    own_expo = jnp.where(visible, jnp.exp(own_scores - own_high), 0.0)
    own_total = jnp.sum(own_expo, axis=2, keepdims=True)
    own_mixed = jnp.einsum("hrn,nd->hrd", own_expo.astype(bf16), own_v, preferred_element_type=f32)
    own_mixed = (own_mixed / own_total).reshape(256, HD)
    own_level = (own_high + jnp.log(own_total)).reshape(1, 256)

    image, qa, qb = lax.optimization_barrier((image, qa, qb))
    w_out, unused = lax.optimization_barrier((w_out, image[0, 0]))
    out_all = lax.all_gather(w_out, "vis", axis=0)
    out_all, text_part = lax.optimization_barrier((out_all, text_part))
    text_sum = lax.psum_scatter(text_part, "vis", scatter_dimension=0, tiled=True)
    text_scale = lax.rsqrt(text_sum[64:65] / D + EPS)
    text_kv = (text_sum[:64] * text_scale).astype(bf16)

    w_pad = jnp.pad(w_qkv.reshape(VD, 3, VHD), ((0, 0), (0, 0), (0, 128 - VHD))).reshape(VD, 384)
    heads = ring_gather(vision(image, vis_gain.reshape(1, VD), w_pad))
    partial = merge(
        ring_owners(vis_index),
        heads,
        image,
        out_all,
        merge_gain.reshape(1, VD),
        w_merge,
        kv_gain.reshape(1, 512),
        w_kv_mine,
    )
    arrived = lax.all_to_all(partial, "vis", split_axis=0, concat_axis=0, tiled=True)
    vis_sum = jnp.sum(arrived.astype(f32), axis=0)
    vis_squares = vis_sum[64:65] + vis_sum[65:66] + vis_sum[66:67]
    vis_kv = (vis_sum[:64] * lax.rsqrt(vis_squares / D + EPS)).astype(bf16)
    vis_kv = lax.all_gather(vis_kv, "vis", axis=0, tiled=True, axis_index_groups=QUADS)
    text_kv = lax.all_gather(text_kv, "vis", axis=0, tiled=True, axis_index_groups=QUADS)

    packed = response(qa, qb, text_kv, mask, vis_kv)
    back = lax.all_to_all(packed, "ctx", split_axis=0, concat_axis=0, tiled=True).astype(f32)
    levels = back[:, 256:258] + back[:, 258:260] + back[:, 260:262]
    levels = levels.reshape(N, 256)
    highest = jnp.maximum(jnp.max(levels, axis=0, keepdims=True), own_level)
    weights = jnp.exp(levels - highest)
    own_weight = jnp.exp(own_level - highest)
    total = jnp.sum(weights, axis=0, keepdims=True) + own_weight
    weights = weights / total
    own_weight = own_weight / total
    result = jnp.sum(back[:, :256] * weights[:, :, None], axis=0)
    result = result + own_mixed * own_weight.reshape(256, 1)
    result = jnp.transpose(result.reshape(2, R_TOK, HD), (1, 0, 2)).reshape(R_TOK, 256)
    live = (positions < resp_len[0])[:, None]
    result = jnp.where(live, result, 0.0).astype(bf16)
    top = lax.all_gather(result[:half], "vis", axis=1, tiled=True)
    bottom = lax.all_gather(result[half:], "vis", axis=1, tiled=True)
    return jnp.concatenate([top, bottom], axis=0)


def solution(mesh):
    return jax.shard_map(
        per_device,
        mesh=mesh,
        in_specs=(
            P(("ctx", "vis"), None),
            P(),
            P(None, "vis"),
            P("vis", None),
            P(),
            P(None, "vis"),
            P(),
            P(),
            P("ctx", "vis"),
            P("vis"),
            P("vis", None),
            P("ctx", None),
            P("ctx", None),
            P("ctx"),
        ),
        out_specs=P("ctx", None),
        check_vma=False,
    )
```

```python
import math

import jax
import jax.numpy as jnp
from jax import lax
from jax.experimental import pallas as pl
from jax.experimental.pallas import tpu as pltpu
from jax.sharding import PartitionSpec as P

VD = 1280
VHEADS = 16
D = 8192
HD = 128
QH = 32
KVH = 4
CROWS = 1024
R_TOK = 128
VHD = 80
GP = 2048
VTOK = 512
N = 16
LOCAL = GP // N
EPS = 1e-06
NEG = -1e30
bf16 = jnp.bfloat16
f32 = jnp.float32

SWAP = [(i, i ^ 1) for i in range(N)]
QUADS = [[4 * g + i for i in range(4)] for g in range(4)]
RING_ORDER = (0, 1, 2, 3, -1, -2, -3, 4)
PIECES = (32, 48)
LOG2E = math.log2(math.e)


def along_z(shift):
    return [(z * 2 + c, ((z + shift) % 8) * 2 + c) for z in range(8) for c in range(2)]


def ring_gather(block):
    pieces = []
    first = 0
    for index, rows in enumerate(PIECES):
        own = block[first : first + rows]
        first += rows
        ups = [own]
        downs = [own]
        for step in range(1, 4):
            ups.append(lax.ppermute(ups[-1], "vis", along_z(1)))
            downs.append(lax.ppermute(downs[-1], "vis", along_z(-1)))
        if index == 0:
            far = lax.ppermute(ups[-1], "vis", along_z(1))
        else:
            far = lax.ppermute(downs[-1], "vis", along_z(-1))
        mine = ups + downs[1:] + [far]
        pieces.append(mine + [lax.ppermute(piece, "vis", SWAP) for piece in mine])
    return [piece for pair in zip(*pieces) for piece in pair]


def ring_owners(vis_index):
    z = vis_index // 2
    core = vis_index % 2
    zs = (z - jnp.array(RING_ORDER, jnp.int32)) % 8
    return jnp.concatenate([zs * 2 + core, zs * 2 + 1 - core])


def dot(a, b, contract):
    return lax.dot_general(a, b, ((contract[:1], contract[1:]), ((), ())), preferred_element_type=f32)


def normed_rows(values, gain):
    center = values - jnp.mean(values, axis=-1, keepdims=True)
    spread = jnp.mean(center * center, axis=-1, keepdims=True)
    return center * lax.rsqrt(spread + EPS) * gain


QKV_STEPS = 4
QKV_ROWS = GP // QKV_STEPS
ATT_STEPS = 2
ATT_ROWS = GP // ATT_STEPS
ATT_PART = 256


def vision_kernel(x_ref, gain_ref, w_ref, out_ref, q_s, k_s, v_s):
    step = pl.program_id(0)

    @pl.when(step < QKV_STEPS)
    def _():
        normed = normed_rows(x_ref[...].astype(f32), gain_ref[...]).astype(bf16)
        qkv = dot(normed, w_ref[...], (1, 0)).astype(bf16)
        rows = pl.ds(pl.multiple_of(step * QKV_ROWS, QKV_ROWS), QKV_ROWS)
        q_s[rows, :] = qkv[:, :128]
        k_s[rows, :] = qkv[:, 128:256]
        lane = lax.broadcasted_iota(jnp.int32, (QKV_ROWS, 128), 1)
        v_s[rows, :] = jnp.where(lane == VHD, jnp.ones((), bf16), qkv[:, 256:])

    @pl.when(step >= QKV_STEPS)
    def _():
        first = pl.multiple_of((step - QKV_STEPS) * ATT_ROWS, ATT_ROWS)
        for part in range(0, ATT_ROWS, ATT_PART):
            query = q_s[pl.ds(first + part, ATT_PART), :]
            scores = dot(query, k_s[...], (1, 1))
            highest = jnp.max(scores, axis=1, keepdims=True)
            expo = jnp.exp2((scores - highest) * (LOG2E / math.sqrt(VHD))).astype(bf16)
            mixed = dot(expo, v_s[...], (1, 0))
            mixed = mixed / mixed[:, VHD : VHD + 1]
            out_ref[:, part : part + ATT_PART] = jnp.transpose(mixed, (1, 0))[:VHD, :].astype(bf16)


def vision(x, gain, w):
    return pl.pallas_call(
        vision_kernel,
        grid=(QKV_STEPS + ATT_STEPS,),
        in_specs=[
            pl.BlockSpec((QKV_ROWS, VD), lambda i: (jnp.minimum(i, QKV_STEPS - 1), 0)),
            pl.BlockSpec((1, VD), lambda i: (0, 0)),
            pl.BlockSpec((VD, 384), lambda i: (0, 0)),
        ],
        out_specs=pl.BlockSpec((VHD, ATT_ROWS), lambda i: (0, jnp.maximum(i - QKV_STEPS, 0))),
        out_shape=jax.ShapeDtypeStruct((VHD, GP), bf16),
        scratch_shapes=[pltpu.VMEM((GP, 128), bf16)] * 3,
        compiler_params=pltpu.CompilerParams(vmem_limit_bytes=40 * 2**20),
        name="vision",
    )(x, gain, w)


MERGE_STEPS = 4
MERGE_ROWS = GP // MERGE_STEPS
MERGE_TOK = VTOK // MERGE_STEPS
CHUNK = 72
HELD = 2 * N


def row_of(column):
    count = column.shape[0]
    down = lax.broadcasted_iota(jnp.int32, (count, count), 0)
    across = lax.broadcasted_iota(jnp.int32, (count, count), 1)
    return jnp.sum(jnp.where(down == across, column, 0.0), axis=0, keepdims=True)


def three_parts(row):
    high = row.astype(bf16).astype(f32)
    middle = (row - high).astype(bf16).astype(f32)
    return high, middle, row - high - middle


def merge_kernel(order_ref, *refs):
    pieces = refs[:HELD]
    x_ref, wo_ref, gain_ref, wm_ref, kg_ref, wk_ref, out_ref, heads_s, merged_s = refs[HELD:]
    step = pl.program_id(0)
    for k in range(N):
        base = order_ref[k] * VHD
        for j, rows in enumerate(PIECES):
            first = pl.multiple_of(base + sum(PIECES[:j]), 16)
            heads_s[pl.ds(first, rows), :] = pieces[len(PIECES) * k + j][...]
    mixed = x_ref[...].astype(f32) + dot(heads_s[...], wo_ref[...], (0, 0))
    merged = normed_rows(mixed, gain_ref[...]).astype(bf16)
    split = merged.reshape(MERGE_ROWS // LOCAL, 4, LOCAL // 4, VD)
    rows = pl.ds(pl.multiple_of(step * MERGE_TOK, MERGE_TOK), MERGE_TOK)
    for a in range(4):
        merged_s[rows, a * VD : (a + 1) * VD] = split[:, a].reshape(MERGE_TOK, VD)

    @pl.when(step == MERGE_STEPS - 1)
    def _():
        visual = dot(merged_s[...], wm_ref[...], (1, 0)).astype(bf16).astype(f32)
        squares = row_of(jnp.sum(visual * visual, axis=1, keepdims=True))
        zeros = jnp.zeros((CHUNK - 67, VTOK), f32)
        extra = jnp.concatenate([*three_parts(squares), zeros], axis=0)
        gained = (visual * kg_ref[...]).astype(bf16)
        kv = dot(wk_ref[...], gained, (0, 1))
        for v in range(N):
            both = jnp.concatenate([kv[64 * v : 64 * v + 64, :], extra], axis=0)
            out_ref[v, :, :] = both.astype(bf16)


def merge(order, pieces, x, w_out, gain, w_merge, kv_gain, w_kv):
    whole = lambda i, order: (0, 0)
    grid_spec = pltpu.PrefetchScalarGridSpec(
        num_scalar_prefetch=1,
        grid=(MERGE_STEPS,),
        in_specs=[
            pl.BlockSpec((piece.shape[0], MERGE_ROWS), lambda i, order: (0, i)) for piece in pieces
        ]
        + [
            pl.BlockSpec((MERGE_ROWS, VD), lambda i, order: (i, 0)),
            pl.BlockSpec((VD, VD), whole),
            pl.BlockSpec((1, VD), whole),
            pl.BlockSpec((4 * VD, 512), whole),
            pl.BlockSpec((1, 512), whole),
            pl.BlockSpec((512, 1024), whole),
        ],
        out_specs=pl.BlockSpec((N, CHUNK, VTOK), lambda i, order: (0, 0, 0)),
        scratch_shapes=[pltpu.VMEM((VD, MERGE_ROWS), bf16), pltpu.VMEM((VTOK, 4 * VD), bf16)],
    )
    return pl.pallas_call(
        merge_kernel,
        grid_spec=grid_spec,
        out_shape=jax.ShapeDtypeStruct((N, CHUNK, VTOK), bf16),
        compiler_params=pltpu.CompilerParams(vmem_limit_bytes=56 * 2**20),
        name="merge",
    )(order, *pieces, x, w_out, gain, w_merge, kv_gain, w_kv)


PACK = 272
PER = 8
SCALE2 = LOG2E / math.sqrt(HD)


def stacked_heads(qa, qb):
    return jnp.concatenate([qa[:, :HD], qb[:, :HD], qa[:, HD:], qb[:, HD:]], axis=0)


def text_kernel(qa_ref, qb_ref, kv_ref, ones_ref, mask_ref, mixed_ref, high_ref):
    values = jnp.concatenate([kv_ref[HD:, :], ones_ref[...]], axis=0)
    for r in range(PER):
        query = stacked_heads(qa_ref[r], qb_ref[r])
        scores = dot(query, kv_ref[:HD, :], (1, 0)) + mask_ref[...]
        highest = jnp.max(scores, axis=1, keepdims=True)
        expo = jnp.exp2((scores - highest) * SCALE2).astype(bf16)
        mixed_ref[r] = dot(expo, values, (1, 1))
        high_ref[r] = jnp.broadcast_to(highest, (2 * R_TOK, HD))


def text_attention(qa, qb, kv, mask):
    whole = lambda i: (0, 0)
    some = lambda i: (i, 0, 0)
    return pl.pallas_call(
        text_kernel,
        grid=(N // PER,),
        in_specs=[
            pl.BlockSpec((PER, R_TOK // 2, 2 * HD), some),
            pl.BlockSpec((PER, R_TOK // 2, 2 * HD), some),
            pl.BlockSpec((2 * HD, CROWS), whole),
            pl.BlockSpec((HD, CROWS), whole),
            pl.BlockSpec((1, CROWS), whole),
        ],
        out_specs=[
            pl.BlockSpec((PER, 2 * R_TOK, 2 * HD), some),
            pl.BlockSpec((PER, 2 * R_TOK, HD), some),
        ],
        out_shape=[
            jax.ShapeDtypeStruct((N, 2 * R_TOK, 2 * HD), f32),
            jax.ShapeDtypeStruct((N, 2 * R_TOK, HD), f32),
        ],
        compiler_params=pltpu.CompilerParams(vmem_limit_bytes=48 * 2**20),
        name="text",
    )(qa, qb, kv, jnp.ones((HD, CROWS), bf16), mask)


def visual_kernel(qa_ref, qb_ref, kv_ref, ones_ref, mixed_ref, high_ref, out_ref):
    values = jnp.concatenate([kv_ref[HD:, :], ones_ref[...]], axis=0)
    for r in range(PER):
        query = stacked_heads(qa_ref[r], qb_ref[r])
        scores = dot(query, kv_ref[:HD, :], (1, 0))
        before = high_ref[r][:, :1]
        highest = jnp.maximum(jnp.max(scores, axis=1, keepdims=True), before)
        expo = jnp.exp2((scores - highest) * SCALE2).astype(bf16)
        mixed = dot(expo, values, (1, 1)) + mixed_ref[r] * jnp.exp2((before - highest) * SCALE2)
        total = mixed[:, HD : HD + 1]
        out_ref[r, : 2 * R_TOK, :] = (mixed[:, :HD] / total).astype(bf16)
        level = row_of(highest * SCALE2 + jnp.log2(total))
        parts = [part[:, k * HD : k * HD + HD] for part in three_parts(level) for k in range(2)]
        tail = jnp.concatenate(parts + [jnp.zeros((10, HD), f32)], axis=0)
        out_ref[r, 2 * R_TOK :, :] = tail.astype(bf16)


def visual_attention(qa, qb, kv, mixed, high):
    whole = lambda i: (0, 0)
    some = lambda i: (i, 0, 0)
    return pl.pallas_call(
        visual_kernel,
        grid=(N // PER,),
        in_specs=[
            pl.BlockSpec((PER, R_TOK // 2, 2 * HD), some),
            pl.BlockSpec((PER, R_TOK // 2, 2 * HD), some),
            pl.BlockSpec((2 * HD, VTOK), whole),
            pl.BlockSpec((HD, VTOK), whole),
            pl.BlockSpec((PER, 2 * R_TOK, 2 * HD), some),
            pl.BlockSpec((PER, 2 * R_TOK, HD), some),
        ],
        out_specs=pl.BlockSpec((PER, PACK, HD), some),
        out_shape=jax.ShapeDtypeStruct((N, PACK, HD), bf16),
        compiler_params=pltpu.CompilerParams(vmem_limit_bytes=48 * 2**20),
        name="visual",
    )(qa, qb, kv, jnp.ones((HD, VTOK), bf16), mixed, high)


def per_device(
    patches,
    vis_gain,
    w_qkv,
    w_out,
    merge_gain,
    w_merge,
    token_dest,
    token_row,
    prompt_text,
    kv_gain,
    w_kv,
    queries,
    resp_kv,
    resp_len,
):
    ctx_index = lax.axis_index("ctx")
    vis_index = lax.axis_index("vis")
    group = vis_index // 4

    local = patches.reshape(LOCAL // 4, 4, VD).transpose(1, 0, 2).reshape(LOCAL, VD)
    image = lax.all_gather(local, "vis", axis=0, tiled=True)

    own_q = lax.dynamic_slice_in_dim(queries, vis_index * 256, 256, 1)
    half = R_TOK // 2
    qa = lax.all_gather(own_q[:half], "ctx", axis=0)
    qb = lax.all_gather(own_q[half:], "ctx", axis=0)

    w_kv_mine = w_kv.reshape(512, 2, KVH, 2, 64).transpose(0, 2, 1, 3, 4).reshape(512, 1024)
    text = prompt_text.astype(f32)
    text_squares = jnp.sum(text * text, axis=1)
    text_gained = (text * kv_gain).astype(bf16)
    text_part = dot(w_kv_mine, text_gained, (0, 1)).reshape(N, 64, CROWS)
    text_extra = jnp.broadcast_to(text_squares[None, None, :], (N, 8, CROWS))
    text_part = jnp.concatenate([text_part, text_extra], axis=1).reshape(N * CHUNK, CROWS)

    flat_dest = token_dest.reshape(-1)
    flat_row = token_row.reshape(-1)
    here = jnp.where(flat_dest == ctx_index, flat_row // 128, -1)
    tall = (here[None, :] == jnp.arange(8, dtype=jnp.int32)[:, None]).astype(bf16)
    wide = ((flat_row % 128)[:, None] == jnp.arange(128, dtype=jnp.int32)[None, :]).astype(bf16)
    taken = dot(tall, wide, (1, 0)).reshape(1, CROWS)
    mask = jnp.where(taken > 0.5, NEG, 0.0)

    own_k = lax.dynamic_slice_in_dim(resp_kv, group * HD, HD, 1)
    own_v = lax.dynamic_slice_in_dim(resp_kv, KVH * HD + group * HD, HD, 1)
    positions = jnp.arange(R_TOK, dtype=jnp.int32)
    visible = positions[None, :] <= positions[:, None]
    q_two = own_q.reshape(R_TOK, 2, HD)
    own_scores = jnp.einsum("rhd,nd->hrn", q_two, own_k, preferred_element_type=f32)
    own_scores = jnp.where(visible, own_scores * (1.0 / math.sqrt(HD)), NEG)
    own_high = jnp.max(own_scores, axis=2, keepdims=True)
    own_expo = jnp.where(visible, jnp.exp(own_scores - own_high), 0.0)
    own_total = jnp.sum(own_expo, axis=2, keepdims=True)
    own_mixed = jnp.einsum("hrn,nd->hrd", own_expo.astype(bf16), own_v, preferred_element_type=f32)
    own_mixed = (own_mixed / own_total).reshape(256, HD)
    own_level = (own_high * LOG2E + jnp.log2(own_total)).reshape(1, 256)

    image, qa, qb, w_out = lax.optimization_barrier((image, qa, qb, w_out))
    out_all = lax.all_gather(w_out, "vis", axis=0, tiled=True)

    w_pad = jnp.pad(w_qkv.reshape(VD, 3, VHD), ((0, 0), (0, 0), (0, 128 - VHD))).reshape(VD, 384)
    own_heads = vision(image, vis_gain.reshape(1, VD), w_pad)
    own_heads, text_part = lax.optimization_barrier((own_heads, text_part))
    text_sum = lax.psum_scatter(text_part, "vis", scatter_dimension=0, tiled=True)
    text_scale = lax.rsqrt(text_sum[64:65] / D + EPS)
    text_kv = (text_sum[:64] * text_scale).astype(bf16)
    text_kv = lax.all_gather(text_kv, "vis", axis=0, tiled=True, axis_index_groups=QUADS)
    text_state = text_attention(qa, qb, text_kv, mask)

    heads = ring_gather(own_heads)
    partial = merge(
        ring_owners(vis_index),
        heads,
        image,
        out_all,
        merge_gain.reshape(1, VD),
        w_merge,
        kv_gain.reshape(1, 512),
        w_kv_mine,
    )
    arrived = lax.all_to_all(partial, "vis", split_axis=0, concat_axis=0, tiled=True)
    arrived, *text_state = lax.optimization_barrier((arrived, *text_state))
    vis_sum = jnp.sum(arrived.astype(f32), axis=0)
    vis_squares = vis_sum[64:65] + vis_sum[65:66] + vis_sum[66:67]
    vis_kv = (vis_sum[:64] * lax.rsqrt(vis_squares / D + EPS)).astype(bf16)
    vis_kv = lax.all_gather(vis_kv, "vis", axis=0, tiled=True, axis_index_groups=QUADS)
    packed = visual_attention(qa, qb, vis_kv, *text_state)
    back = lax.all_to_all(packed, "ctx", split_axis=0, concat_axis=0, tiled=True).astype(f32)
    levels = back[:, 256:258] + back[:, 258:260] + back[:, 260:262]
    levels = levels.reshape(N, 256)
    highest = jnp.maximum(jnp.max(levels, axis=0, keepdims=True), own_level)
    weights = jnp.exp2(levels - highest)
    own_weight = jnp.exp2(own_level - highest)
    total = jnp.sum(weights, axis=0, keepdims=True) + own_weight
    weights = weights / total
    own_weight = own_weight / total
    result = jnp.sum(back[:, :256] * weights[:, :, None], axis=0)
    result = result + own_mixed * own_weight.reshape(256, 1)
    result = jnp.transpose(result.reshape(2, R_TOK, HD), (1, 0, 2)).reshape(R_TOK, 256)
    live = (positions < resp_len[0])[:, None]
    result = jnp.where(live, result, 0.0).astype(bf16)
    top = lax.all_gather(result[:half], "vis", axis=1, tiled=True)
    bottom = lax.all_gather(result[half:], "vis", axis=1, tiled=True)
    return jnp.concatenate([top, bottom], axis=0)


def solution(mesh):
    return jax.shard_map(
        per_device,
        mesh=mesh,
        in_specs=(
            P(("ctx", "vis"), None),
            P(),
            P(None, "vis"),
            P("vis", None),
            P(),
            P(None, "vis"),
            P(),
            P(),
            P("ctx", "vis"),
            P("vis"),
            P("vis", None),
            P("ctx", None),
            P("ctx", None),
            P("ctx"),
        ),
        out_specs=P("ctx", None),
        check_vma=False,
    )
```

```python
import math

import jax
import jax.numpy as jnp
from jax import lax
from jax.experimental import pallas as pl
from jax.experimental.pallas import tpu as pltpu
from jax.sharding import PartitionSpec as P

VD = 1280
VHEADS = 16
D = 8192
HD = 128
QH = 32
KVH = 4
CROWS = 1024
R_TOK = 128
VHD = 80
GP = 2048
VTOK = 512
N = 16
LOCAL = GP // N
EPS = 1e-06
NEG = -1e30
bf16 = jnp.bfloat16
f32 = jnp.float32

QUADS = [[4 * g + i for i in range(4)] for g in range(4)]
LOG2E = math.log2(math.e)


def onward(block):
    pairs = [(2 * z, 2 * ((z + 1) % 8)) for z in range(8)]
    pairs += [(2 * z + 1, 2 * ((z - 1) % 8) + 1) for z in range(8)]
    return lax.ppermute(block, "vis", pairs)


def swapped(block):
    return lax.ppermute(block, "vis", [(i, i ^ 1) for i in range(N)])


def ring_gather(block):
    same = [block]
    other = [swapped(block)]
    for step in range(3):
        same.append(onward(same[-1]))
        other.append(onward(other[-1]))
    same.append(onward(same[-1]))
    away = [swapped(piece) for piece in same[1:]]
    back = [swapped(piece) for piece in other[1:]]
    return same + other + away + back


def ring_owners(vis_index):
    z = vis_index // 2
    core = vis_index % 2
    sign = 2 * core - 1
    hops = jnp.array((0, 1, 2, 3, 4, 0, 1, 2, 3, -1, -2, -3, -4, -1, -2, -3), jnp.int32)
    flips = jnp.array((0,) * 5 + (1,) * 4 + (1,) * 4 + (0,) * 3, jnp.int32)
    return (z + sign * hops) % 8 * 2 + (core + flips) % 2


def dot(a, b, contract):
    return lax.dot_general(a, b, ((contract[:1], contract[1:]), ((), ())), preferred_element_type=f32)


def normed_rows(values, gain):
    center = values - jnp.mean(values, axis=-1, keepdims=True)
    spread = jnp.mean(center * center, axis=-1, keepdims=True)
    return center * lax.rsqrt(spread + EPS) * gain


QKV_STEPS = 4
QKV_ROWS = GP // QKV_STEPS
ATT_STEPS = 2
ATT_ROWS = GP // ATT_STEPS
ATT_PART = 256


def vision_kernel(x_ref, gain_ref, w_ref, out_ref, q_s, k_s, v_s):
    step = pl.program_id(0)

    @pl.when(step < QKV_STEPS)
    def _():
        rows = x_ref[...].reshape(QKV_ROWS, VD)
        normed = normed_rows(rows.astype(f32), gain_ref[...]).astype(bf16)
        qkv = dot(normed, w_ref[...], (1, 0)).astype(bf16)
        rows = pl.ds(pl.multiple_of(step * QKV_ROWS, QKV_ROWS), QKV_ROWS)
        q_s[rows, :] = qkv[:, :128]
        k_s[rows, :] = qkv[:, 128:256]
        lane = lax.broadcasted_iota(jnp.int32, (QKV_ROWS, 128), 1)
        v_s[rows, :] = jnp.where(lane == VHD, jnp.ones((), bf16), qkv[:, 256:])

    @pl.when(step >= QKV_STEPS)
    def _():
        first = pl.multiple_of((step - QKV_STEPS) * ATT_ROWS, ATT_ROWS)
        for part in range(0, ATT_ROWS, ATT_PART):
            query = q_s[pl.ds(first + part, ATT_PART), :]
            scores = dot(query, k_s[...], (1, 1))
            highest = jnp.max(scores, axis=1, keepdims=True)
            expo = jnp.exp2((scores - highest) * (LOG2E / math.sqrt(VHD))).astype(bf16)
            mixed = dot(expo, v_s[...], (1, 0))
            mixed = mixed / mixed[:, VHD : VHD + 1]
            out_ref[:, part : part + ATT_PART] = jnp.transpose(mixed, (1, 0))[:VHD, :].astype(bf16)


def vision(x, gain, w):
    return pl.pallas_call(
        vision_kernel,
        grid=(QKV_STEPS + ATT_STEPS,),
        in_specs=[
            pl.BlockSpec((N // QKV_STEPS, LOCAL, VD), lambda i: (jnp.minimum(i, QKV_STEPS - 1), 0, 0)),
            pl.BlockSpec((1, VD), lambda i: (0, 0)),
            pl.BlockSpec((VD, 384), lambda i: (0, 0)),
        ],
        out_specs=pl.BlockSpec((VHD, ATT_ROWS), lambda i: (0, jnp.maximum(i - QKV_STEPS, 0))),
        out_shape=jax.ShapeDtypeStruct((VHD, GP), bf16),
        scratch_shapes=[pltpu.VMEM((GP, 128), bf16)] * 3,
        compiler_params=pltpu.CompilerParams(vmem_limit_bytes=40 * 2**20),
        name="vision",
    )(x, gain, w)


MERGE_STEPS = 4
MERGE_ROWS = GP // MERGE_STEPS
MERGE_TOK = VTOK // MERGE_STEPS
CHUNK = 72
HELD = N


def row_of(column):
    count = column.shape[0]
    down = lax.broadcasted_iota(jnp.int32, (count, count), 0)
    across = lax.broadcasted_iota(jnp.int32, (count, count), 1)
    return jnp.sum(jnp.where(down == across, column, 0.0), axis=0, keepdims=True)


def three_parts(row):
    high = row.astype(bf16).astype(f32)
    middle = (row - high).astype(bf16).astype(f32)
    return high, middle, row - high - middle


def merge_kernel(order_ref, *refs):
    pieces = refs[:HELD]
    x_ref, all_ref, gain_ref, wm_ref, kg_ref, wk_ref, out_ref, heads_s, merged_s, wo_s, sems = refs[HELD:]
    step = pl.program_id(0)

    def fetch(k):
        source = all_ref.at[k, pl.ds(LOCAL, VHD), :]
        return pltpu.make_async_copy(source, wo_s.at[pl.ds(k * VHD, VHD), :], sems.at[k])

    @pl.when(step == 0)
    def _():
        for k in range(N):
            fetch(k).start()

    for k in range(N):
        first = pl.multiple_of(order_ref[k] * VHD, VHD)
        heads_s[pl.ds(first, VHD), :] = pieces[k][...]

    @pl.when(step == 0)
    def _():
        for k in range(N):
            fetch(k).wait()

    floats = x_ref[...].reshape(MERGE_ROWS, VD).astype(f32)
    mixed = floats + dot(heads_s[...], wo_s[...], (0, 0))
    merged = normed_rows(mixed, gain_ref[...]).astype(bf16)
    split = merged.reshape(MERGE_ROWS // LOCAL, 4, LOCAL // 4, VD)
    rows = pl.ds(pl.multiple_of(step * MERGE_TOK, MERGE_TOK), MERGE_TOK)
    for a in range(4):
        merged_s[rows, a * VD : (a + 1) * VD] = split[:, a].reshape(MERGE_TOK, VD)

    @pl.when(step == MERGE_STEPS - 1)
    def _():
        visual = dot(merged_s[...], wm_ref[...], (1, 0)).astype(bf16).astype(f32)
        squares = row_of(jnp.sum(visual * visual, axis=1, keepdims=True))
        zeros = jnp.zeros((CHUNK - 67, VTOK), f32)
        extra = jnp.concatenate([*three_parts(squares), zeros], axis=0)
        gained = (visual * kg_ref[...]).astype(bf16)
        kv = dot(wk_ref[...], gained, (0, 1))
        for v in range(N):
            both = jnp.concatenate([kv[64 * v : 64 * v + 64, :], extra], axis=0)
            out_ref[v, :, :] = both.astype(bf16)


def merge(order, pieces, x, gain, w_merge, kv_gain, w_kv):
    whole = lambda i, order: (0, 0)
    grid_spec = pltpu.PrefetchScalarGridSpec(
        num_scalar_prefetch=1,
        grid=(MERGE_STEPS,),
        in_specs=[
            pl.BlockSpec((piece.shape[0], MERGE_ROWS), lambda i, order: (0, i)) for piece in pieces
        ]
        + [
            pl.BlockSpec((N // MERGE_STEPS, LOCAL, VD), lambda i, order: (i, 0, 0)),
            pl.BlockSpec(memory_space=pl.ANY),
            pl.BlockSpec((1, VD), whole),
            pl.BlockSpec((4 * VD, 512), whole),
            pl.BlockSpec((1, 512), whole),
            pl.BlockSpec((512, 1024), whole),
        ],
        out_specs=pl.BlockSpec((N, CHUNK, VTOK), lambda i, order: (0, 0, 0)),
        scratch_shapes=[
            pltpu.VMEM((VD, MERGE_ROWS), bf16),
            pltpu.VMEM((VTOK, 4 * VD), bf16),
            pltpu.VMEM((VD, VD), bf16),
            pltpu.SemaphoreType.DMA((N,)),
        ],
    )
    return pl.pallas_call(
        merge_kernel,
        grid_spec=grid_spec,
        out_shape=jax.ShapeDtypeStruct((N, CHUNK, VTOK), bf16),
        compiler_params=pltpu.CompilerParams(vmem_limit_bytes=56 * 2**20),
        name="merge",
    )(order, *pieces, x, x, gain, w_merge, kv_gain, w_kv)


PACK = 272
PER = 8
SCALE2 = LOG2E / math.sqrt(HD)


def stacked_heads(qa, qb):
    return jnp.concatenate([qa[:, :HD], qb[:, :HD], qa[:, HD:], qb[:, HD:]], axis=0)


def text_kernel(qa_ref, qb_ref, kv_ref, ones_ref, mask_ref, mixed_ref, high_ref):
    values = jnp.concatenate([kv_ref[HD:, :], ones_ref[...]], axis=0)
    for r in range(PER):
        query = stacked_heads(qa_ref[r], qb_ref[r])
        scores = dot(query, kv_ref[:HD, :], (1, 0)) + mask_ref[...]
        highest = jnp.max(scores, axis=1, keepdims=True)
        expo = jnp.exp2((scores - highest) * SCALE2).astype(bf16)
        mixed_ref[r] = dot(expo, values, (1, 1))
        high_ref[r] = jnp.broadcast_to(highest, (2 * R_TOK, HD))


def text_attention(qa, qb, kv, mask):
    whole = lambda i: (0, 0)
    some = lambda i: (i, 0, 0)
    return pl.pallas_call(
        text_kernel,
        grid=(N // PER,),
        in_specs=[
            pl.BlockSpec((PER, R_TOK // 2, 2 * HD), some),
            pl.BlockSpec((PER, R_TOK // 2, 2 * HD), some),
            pl.BlockSpec((2 * HD, CROWS), whole),
            pl.BlockSpec((HD, CROWS), whole),
            pl.BlockSpec((1, CROWS), whole),
        ],
        out_specs=[
            pl.BlockSpec((PER, 2 * R_TOK, 2 * HD), some),
            pl.BlockSpec((PER, 2 * R_TOK, HD), some),
        ],
        out_shape=[
            jax.ShapeDtypeStruct((N, 2 * R_TOK, 2 * HD), f32),
            jax.ShapeDtypeStruct((N, 2 * R_TOK, HD), f32),
        ],
        compiler_params=pltpu.CompilerParams(vmem_limit_bytes=48 * 2**20),
        name="text",
    )(qa, qb, kv, jnp.ones((HD, CROWS), bf16), mask)


def visual_kernel(qa_ref, qb_ref, kv_ref, ones_ref, mixed_ref, high_ref, out_ref):
    values = jnp.concatenate([kv_ref[HD:, :], ones_ref[...]], axis=0)
    for r in range(PER):
        query = stacked_heads(qa_ref[r], qb_ref[r])
        scores = dot(query, kv_ref[:HD, :], (1, 0))
        before = high_ref[r][:, :1]
        highest = jnp.maximum(jnp.max(scores, axis=1, keepdims=True), before)
        expo = jnp.exp2((scores - highest) * SCALE2).astype(bf16)
        mixed = dot(expo, values, (1, 1)) + mixed_ref[r] * jnp.exp2((before - highest) * SCALE2)
        total = mixed[:, HD : HD + 1]
        out_ref[r, : 2 * R_TOK, :] = (mixed[:, :HD] / total).astype(bf16)
        level = row_of(highest * SCALE2 + jnp.log2(total))
        parts = [part[:, k * HD : k * HD + HD] for part in three_parts(level) for k in range(2)]
        tail = jnp.concatenate(parts + [jnp.zeros((10, HD), f32)], axis=0)
        out_ref[r, 2 * R_TOK :, :] = tail.astype(bf16)


def visual_attention(qa, qb, kv, mixed, high):
    whole = lambda i: (0, 0)
    some = lambda i: (i, 0, 0)
    return pl.pallas_call(
        visual_kernel,
        grid=(N // PER,),
        in_specs=[
            pl.BlockSpec((PER, R_TOK // 2, 2 * HD), some),
            pl.BlockSpec((PER, R_TOK // 2, 2 * HD), some),
            pl.BlockSpec((2 * HD, VTOK), whole),
            pl.BlockSpec((HD, VTOK), whole),
            pl.BlockSpec((PER, 2 * R_TOK, 2 * HD), some),
            pl.BlockSpec((PER, 2 * R_TOK, HD), some),
        ],
        out_specs=pl.BlockSpec((PER, PACK, HD), some),
        out_shape=jax.ShapeDtypeStruct((N, PACK, HD), bf16),
        compiler_params=pltpu.CompilerParams(vmem_limit_bytes=48 * 2**20),
        name="visual",
    )(qa, qb, kv, jnp.ones((HD, VTOK), bf16), mixed, high)


def place_kernel(order_ref, *refs):
    out_ref = refs[-1]
    for k in range(N):
        first = pl.multiple_of(order_ref[k] * 2 * HD, 2 * HD)
        out_ref[:, pl.ds(first, 2 * HD)] = refs[k][...]


def placed(order, pieces):
    whole = lambda i, order: (0, 0)
    grid_spec = pltpu.PrefetchScalarGridSpec(
        num_scalar_prefetch=1,
        grid=(1,),
        in_specs=[pl.BlockSpec((R_TOK, 2 * HD), whole)] * N,
        out_specs=pl.BlockSpec((R_TOK, QH * HD), whole),
    )
    return pl.pallas_call(
        place_kernel,
        grid_spec=grid_spec,
        out_shape=jax.ShapeDtypeStruct((R_TOK, QH * HD), bf16),
        name="placed",
    )(order, *pieces)


def per_device(
    patches,
    vis_gain,
    w_qkv,
    w_out,
    merge_gain,
    w_merge,
    token_dest,
    token_row,
    prompt_text,
    kv_gain,
    w_kv,
    queries,
    resp_kv,
    resp_len,
):
    ctx_index = lax.axis_index("ctx")
    vis_index = lax.axis_index("vis")
    group = vis_index // 4

    local = patches.reshape(LOCAL // 4, 4, VD).transpose(1, 0, 2).reshape(LOCAL, VD)
    image = lax.all_gather(jnp.concatenate([local, w_out], axis=0), "vis", axis=0)
    w_pad = jnp.pad(w_qkv.reshape(VD, 3, VHD), ((0, 0), (0, 0), (0, 128 - VHD))).reshape(VD, 384)

    w_kv_mine = w_kv.reshape(512, 2, KVH, 2, 64).transpose(0, 2, 1, 3, 4).reshape(512, 1024)
    text = prompt_text.astype(f32)
    text_squares = jnp.sum(text * text, axis=1)
    text_gained = (text * kv_gain).astype(bf16)
    text_part = dot(w_kv_mine, text_gained, (0, 1)).reshape(N, 64, CROWS)
    text_extra = jnp.broadcast_to(text_squares[None, None, :], (N, 8, CROWS))
    text_part = jnp.concatenate([text_part, text_extra], axis=1).reshape(N * CHUNK, CROWS)

    own_q = lax.dynamic_slice_in_dim(queries, vis_index * 256, 256, 1)
    own_q, text_part, w_pad = lax.optimization_barrier((own_q, text_part, w_pad))
    half = R_TOK // 2
    qa = lax.all_gather(own_q[:half], "ctx", axis=0)
    qb = lax.all_gather(own_q[half:], "ctx", axis=0)

    flat_dest = token_dest.reshape(-1)
    flat_row = token_row.reshape(-1)
    here = jnp.where(flat_dest == ctx_index, flat_row // 128, -1)
    tall = (here[None, :] == jnp.arange(8, dtype=jnp.int32)[:, None]).astype(bf16)
    wide = ((flat_row % 128)[:, None] == jnp.arange(128, dtype=jnp.int32)[None, :]).astype(bf16)
    taken = dot(tall, wide, (1, 0)).reshape(1, CROWS)
    mask = jnp.where(taken > 0.5, NEG, 0.0)

    own_k = lax.dynamic_slice_in_dim(resp_kv, group * HD, HD, 1)
    own_v = lax.dynamic_slice_in_dim(resp_kv, KVH * HD + group * HD, HD, 1)
    positions = jnp.arange(R_TOK, dtype=jnp.int32)
    visible = positions[None, :] <= positions[:, None]
    q_two = own_q.reshape(R_TOK, 2, HD)
    own_scores = jnp.einsum("rhd,nd->hrn", q_two, own_k, preferred_element_type=f32)
    own_scores = jnp.where(visible, own_scores * (1.0 / math.sqrt(HD)), NEG)
    own_high = jnp.max(own_scores, axis=2, keepdims=True)
    own_expo = jnp.where(visible, jnp.exp(own_scores - own_high), 0.0)
    own_total = jnp.sum(own_expo, axis=2, keepdims=True)
    own_mixed = jnp.einsum("hrn,nd->hrd", own_expo.astype(bf16), own_v, preferred_element_type=f32)
    own_mixed = (own_mixed / own_total).reshape(256, HD)
    own_level = (own_high * LOG2E + jnp.log2(own_total)).reshape(1, 256)

    image, qa, qb, text_part = lax.optimization_barrier((image, qa, qb, text_part))
    own_heads = vision(image, vis_gain.reshape(1, VD), w_pad)
    text_sum = lax.psum_scatter(text_part, "vis", scatter_dimension=0, tiled=True)
    text_scale = lax.rsqrt(text_sum[64:65] / D + EPS)
    text_kv = (text_sum[:64] * text_scale).astype(bf16)
    text_kv = lax.all_gather(text_kv, "vis", axis=0, tiled=True, axis_index_groups=QUADS)
    text_state = text_attention(qa, qb, text_kv, mask)

    owners = ring_owners(vis_index)
    partial = merge(
        owners,
        ring_gather(own_heads),
        image,
        merge_gain.reshape(1, VD),
        w_merge,
        kv_gain.reshape(1, 512),
        w_kv_mine,
    )
    arrived = lax.all_to_all(partial, "vis", split_axis=0, concat_axis=0, tiled=True)
    arrived, *text_state = lax.optimization_barrier((arrived, *text_state))
    vis_sum = jnp.sum(arrived.astype(f32), axis=0)
    vis_squares = vis_sum[64:65] + vis_sum[65:66] + vis_sum[66:67]
    vis_kv = (vis_sum[:64] * lax.rsqrt(vis_squares / D + EPS)).astype(bf16)
    vis_kv = lax.all_gather(vis_kv, "vis", axis=0, tiled=True, axis_index_groups=QUADS)
    packed = visual_attention(qa, qb, vis_kv, *text_state)
    back = lax.all_to_all(packed, "ctx", split_axis=0, concat_axis=0, tiled=True).astype(f32)
    levels = back[:, 256:258] + back[:, 258:260] + back[:, 260:262]
    levels = levels.reshape(N, 256)
    highest = jnp.maximum(jnp.max(levels, axis=0, keepdims=True), own_level)
    weights = jnp.exp2(levels - highest)
    own_weight = jnp.exp2(own_level - highest)
    total = jnp.sum(weights, axis=0, keepdims=True) + own_weight
    weights = weights / total
    own_weight = own_weight / total
    result = jnp.sum(back[:, :256] * weights[:, :, None], axis=0)
    result = result + own_mixed * own_weight.reshape(256, 1)
    result = jnp.transpose(result.reshape(2, R_TOK, HD), (1, 0, 2)).reshape(R_TOK, 256)
    live = (positions < resp_len[0])[:, None]
    result = jnp.where(live, result, 0.0).astype(bf16)
    return placed(owners, ring_gather(result))


def solution(mesh):
    return jax.shard_map(
        per_device,
        mesh=mesh,
        in_specs=(
            P(("ctx", "vis"), None),
            P(),
            P(None, "vis"),
            P("vis", None),
            P(),
            P(None, "vis"),
            P(),
            P(),
            P("ctx", "vis"),
            P("vis"),
            P("vis", None),
            P("ctx", None),
            P("ctx", None),
            P("ctx"),
        ),
        out_specs=P("ctx", None),
        check_vma=False,
    )
```

```python
import math

import jax
import jax.numpy as jnp
from jax import lax
from jax.experimental import pallas as pl
from jax.experimental.pallas import tpu as pltpu
from jax.sharding import PartitionSpec as P

VD = 1280
VHEADS = 16
D = 8192
HD = 128
QH = 32
KVH = 4
CROWS = 1024
R_TOK = 128
VHD = 80
GP = 2048
VTOK = 512
N = 16
LOCAL = GP // N
EPS = 1e-06
NEG = -1e30
bf16 = jnp.bfloat16
f32 = jnp.float32

QUADS = [[4 * g + i for i in range(4)] for g in range(4)]
LOG2E = math.log2(math.e)


def onward(block):
    pairs = [(2 * z, 2 * ((z + 1) % 8)) for z in range(8)]
    pairs += [(2 * z + 1, 2 * ((z - 1) % 8) + 1) for z in range(8)]
    return lax.ppermute(block, "vis", pairs)


def swapped(block):
    return lax.ppermute(block, "vis", [(i, i ^ 1) for i in range(N)])


def ring_gather(block):
    same = [block]
    other = [swapped(block)]
    for step in range(3):
        same.append(onward(same[-1]))
        other.append(onward(other[-1]))
    same.append(onward(same[-1]))
    away = [swapped(piece) for piece in same[1:]]
    back = [swapped(piece) for piece in other[1:]]
    return same + other + away + back


def ring_owners(vis_index):
    z = vis_index // 2
    core = vis_index % 2
    sign = 2 * core - 1
    hops = jnp.array((0, 1, 2, 3, 4, 0, 1, 2, 3, -1, -2, -3, -4, -1, -2, -3), jnp.int32)
    flips = jnp.array((0,) * 5 + (1,) * 4 + (1,) * 4 + (0,) * 3, jnp.int32)
    return (z + sign * hops) % 8 * 2 + (core + flips) % 2


def dot(a, b, contract):
    return lax.dot_general(a, b, ((contract[:1], contract[1:]), ((), ())), preferred_element_type=f32)


def normed_rows(values, gain):
    center = values - jnp.mean(values, axis=-1, keepdims=True)
    spread = jnp.mean(center * center, axis=-1, keepdims=True)
    return center * lax.rsqrt(spread + EPS) * gain


QKV_STEPS = 4
QKV_ROWS = GP // QKV_STEPS
ATT_STEPS = 2
ATT_ROWS = GP // ATT_STEPS
ATT_PART = 256


def vision_kernel(order_ref, *refs):
    pieces = refs[:N]
    gain_ref, w_ref, out_ref, image_ref, x_s, q_s, k_s, v_s, in_sems, out_sem = refs[N:]
    step = pl.program_id(0)
    whole = pltpu.make_async_copy(x_s, image_ref, out_sem)

    @pl.when(step == 0)
    def _():
        copies = [
            pltpu.make_async_copy(pieces[k], x_s.at[order_ref[k]], in_sems.at[k]) for k in range(N)
        ]
        for copy in copies:
            copy.start()
        for copy in copies:
            copy.wait()
        whole.start()

    @pl.when(step < QKV_STEPS)
    def _():
        count = N // QKV_STEPS
        rows = x_s[pl.ds(step * count, count)].reshape(QKV_ROWS, VD)
        normed = normed_rows(rows.astype(f32), gain_ref[...]).astype(bf16)
        qkv = dot(normed, w_ref[...], (1, 0)).astype(bf16)
        rows = pl.ds(pl.multiple_of(step * QKV_ROWS, QKV_ROWS), QKV_ROWS)
        q_s[rows, :] = qkv[:, :128]
        k_s[rows, :] = qkv[:, 128:256]
        lane = lax.broadcasted_iota(jnp.int32, (QKV_ROWS, 128), 1)
        v_s[rows, :] = jnp.where(lane == VHD, jnp.ones((), bf16), qkv[:, 256:])

    @pl.when(step >= QKV_STEPS)
    def _():
        first = pl.multiple_of((step - QKV_STEPS) * ATT_ROWS, ATT_ROWS)
        for part in range(0, ATT_ROWS, ATT_PART):
            query = q_s[pl.ds(first + part, ATT_PART), :]
            scores = dot(query, k_s[...], (1, 1))
            highest = jnp.max(scores, axis=1, keepdims=True)
            expo = jnp.exp2((scores - highest) * (LOG2E / math.sqrt(VHD))).astype(bf16)
            mixed = dot(expo, v_s[...], (1, 0))
            mixed = mixed / mixed[:, VHD : VHD + 1]
            out_ref[:, part : part + ATT_PART] = jnp.transpose(mixed, (1, 0))[:VHD, :].astype(bf16)

    @pl.when(step == QKV_STEPS + ATT_STEPS - 1)
    def _():
        whole.wait()


def vision(order, pieces, gain, w):
    whole = lambda i, order: (0, 0)
    grid_spec = pltpu.PrefetchScalarGridSpec(
        num_scalar_prefetch=1,
        grid=(QKV_STEPS + ATT_STEPS,),
        in_specs=[pl.BlockSpec(memory_space=pl.ANY)] * N
        + [pl.BlockSpec((1, VD), whole), pl.BlockSpec((VD, 384), whole)],
        out_specs=[
            pl.BlockSpec((VHD, ATT_ROWS), lambda i, order: (0, jnp.maximum(i - QKV_STEPS, 0))),
            pl.BlockSpec(memory_space=pl.ANY),
        ],
        scratch_shapes=[pltpu.VMEM((N, LOCAL, VD), bf16)]
        + [pltpu.VMEM((GP, 128), bf16)] * 3
        + [pltpu.SemaphoreType.DMA((N,)), pltpu.SemaphoreType.DMA],
    )
    return pl.pallas_call(
        vision_kernel,
        grid_spec=grid_spec,
        out_shape=[
            jax.ShapeDtypeStruct((VHD, GP), bf16),
            jax.ShapeDtypeStruct((N, LOCAL, VD), bf16),
        ],
        compiler_params=pltpu.CompilerParams(vmem_limit_bytes=40 * 2**20),
        name="vision",
    )(order, *pieces, gain, w)


MERGE_STEPS = 4
MERGE_ROWS = GP // MERGE_STEPS
MERGE_TOK = VTOK // MERGE_STEPS
CHUNK = 72
HELD = N
WIDE = 256


def row_of(column):
    count = column.shape[0]
    down = lax.broadcasted_iota(jnp.int32, (count, count), 0)
    across = lax.broadcasted_iota(jnp.int32, (count, count), 1)
    return jnp.sum(jnp.where(down == across, column, 0.0), axis=0, keepdims=True)


def three_parts(row):
    high = row.astype(bf16).astype(f32)
    middle = (row - high).astype(bf16).astype(f32)
    return high, middle, row - high - middle


def merge_kernel(order_ref, *refs):
    pieces = refs[:HELD]
    x_ref, all_ref, gain_ref, wm_ref, kg_ref, wk_ref, out_ref, heads_s, merged_s, wo_s, sems = refs[HELD:]
    step = pl.program_id(0)

    def fetch(k, j):
        source = all_ref.at[k, pl.ds(R_TOK + j * VHD, VHD), :]
        target = wo_s.at[pl.ds(k * VHD, VHD), pl.ds(j * WIDE, WIDE)]
        return pltpu.make_async_copy(source, target, sems.at[k, j])

    @pl.when(step == 0)
    def _():
        for k in range(N):
            for j in range(VD // WIDE):
                fetch(k, j).start()

    for k in range(N):
        first = pl.multiple_of(order_ref[k] * VHD, VHD)
        heads_s[pl.ds(first, VHD), :] = pieces[k][...]

    @pl.when(step == 0)
    def _():
        for k in range(N):
            for j in range(VD // WIDE):
                fetch(k, j).wait()

    floats = x_ref[...].reshape(MERGE_ROWS, VD).astype(f32)
    mixed = floats + dot(heads_s[...], wo_s[...], (0, 0))
    merged = normed_rows(mixed, gain_ref[...]).astype(bf16)
    split = merged.reshape(MERGE_ROWS // LOCAL, 4, LOCAL // 4, VD)
    rows = pl.ds(pl.multiple_of(step * MERGE_TOK, MERGE_TOK), MERGE_TOK)
    for a in range(4):
        merged_s[rows, a * VD : (a + 1) * VD] = split[:, a].reshape(MERGE_TOK, VD)

    @pl.when(step == MERGE_STEPS - 1)
    def _():
        visual = dot(merged_s[...], wm_ref[...], (1, 0)).astype(bf16).astype(f32)
        squares = row_of(jnp.sum(visual * visual, axis=1, keepdims=True))
        zeros = jnp.zeros((CHUNK - 67, VTOK), f32)
        extra = jnp.concatenate([*three_parts(squares), zeros], axis=0)
        gained = (visual * kg_ref[...]).astype(bf16)
        kv = dot(wk_ref[...], gained, (0, 1))
        for v in range(N):
            both = jnp.concatenate([kv[64 * v : 64 * v + 64, :], extra], axis=0)
            out_ref[v, :, :] = both.astype(bf16)


def merge(order, pieces, x, shared, gain, w_merge, kv_gain, w_kv):
    whole = lambda i, order: (0, 0)
    grid_spec = pltpu.PrefetchScalarGridSpec(
        num_scalar_prefetch=1,
        grid=(MERGE_STEPS,),
        in_specs=[
            pl.BlockSpec((piece.shape[0], MERGE_ROWS), lambda i, order: (0, i)) for piece in pieces
        ]
        + [
            pl.BlockSpec((N // MERGE_STEPS, LOCAL, VD), lambda i, order: (i, 0, 0)),
            pl.BlockSpec(memory_space=pl.ANY),
            pl.BlockSpec((1, VD), whole),
            pl.BlockSpec((4 * VD, 512), whole),
            pl.BlockSpec((1, 512), whole),
            pl.BlockSpec((512, 1024), whole),
        ],
        out_specs=pl.BlockSpec((N, CHUNK, VTOK), lambda i, order: (0, 0, 0)),
        scratch_shapes=[
            pltpu.VMEM((VD, MERGE_ROWS), bf16),
            pltpu.VMEM((VTOK, 4 * VD), bf16),
            pltpu.VMEM((VD, VD), bf16),
            pltpu.SemaphoreType.DMA((N, VD // WIDE)),
        ],
    )
    return pl.pallas_call(
        merge_kernel,
        grid_spec=grid_spec,
        out_shape=jax.ShapeDtypeStruct((N, CHUNK, VTOK), bf16),
        compiler_params=pltpu.CompilerParams(vmem_limit_bytes=56 * 2**20),
        name="merge",
    )(order, *pieces, x, shared, gain, w_merge, kv_gain, w_kv)


PACK = 272
PER = 8
SCALE2 = LOG2E / math.sqrt(HD)


def response_kernel(q_ref, kv_ref, ones_ref, mask_ref, out_ref):
    values = jnp.concatenate([kv_ref[HD:, :], ones_ref[...]], axis=0)
    for r in range(PER):
        query = jnp.concatenate([q_ref[r, :, :HD], q_ref[r, :, HD:]], axis=0)
        scores = dot(query, kv_ref[:HD, :], (1, 0)) + mask_ref[...]
        highest = jnp.max(scores, axis=1, keepdims=True)
        expo = jnp.exp2((scores - highest) * SCALE2).astype(bf16)
        mixed = dot(expo, values, (1, 1))
        total = mixed[:, HD : HD + 1]
        out_ref[r, : 2 * R_TOK, :] = (mixed[:, :HD] / total).astype(bf16)
        level = row_of(highest * SCALE2 + jnp.log2(total))
        parts = [part[:, k * HD : k * HD + HD] for part in three_parts(level) for k in range(2)]
        tail = jnp.concatenate(parts + [jnp.zeros((10, HD), f32)], axis=0)
        out_ref[r, 2 * R_TOK :, :] = tail.astype(bf16)


def response(shared, kv, mask):
    whole = lambda i: (0, 0)
    some = lambda i: (i, 0, 0)
    keys = CROWS + VTOK
    return pl.pallas_call(
        response_kernel,
        grid=(N // PER,),
        in_specs=[
            pl.BlockSpec((PER, R_TOK, 2 * HD), some),
            pl.BlockSpec((2 * HD, keys), whole),
            pl.BlockSpec((HD, keys), whole),
            pl.BlockSpec((1, keys), whole),
        ],
        out_specs=pl.BlockSpec((PER, PACK, HD), some),
        out_shape=jax.ShapeDtypeStruct((N, PACK, HD), bf16),
        compiler_params=pltpu.CompilerParams(vmem_limit_bytes=48 * 2**20),
        name="response",
    )(shared, kv, jnp.ones((HD, keys), bf16), mask)


def place_kernel(order_ref, *refs):
    out_ref = refs[-1]
    for k in range(N):
        first = pl.multiple_of(order_ref[k] * 2 * HD, 2 * HD)
        out_ref[:, pl.ds(first, 2 * HD)] = refs[k][...]


def placed(order, pieces):
    whole = lambda i, order: (0, 0)
    grid_spec = pltpu.PrefetchScalarGridSpec(
        num_scalar_prefetch=1,
        grid=(1,),
        in_specs=[pl.BlockSpec((R_TOK, 2 * HD), whole)] * N,
        out_specs=pl.BlockSpec((R_TOK, QH * HD), whole),
    )
    return pl.pallas_call(
        place_kernel,
        grid_spec=grid_spec,
        out_shape=jax.ShapeDtypeStruct((R_TOK, QH * HD), bf16),
        name="placed",
    )(order, *pieces)


def per_device(
    patches,
    vis_gain,
    w_qkv,
    w_out,
    merge_gain,
    w_merge,
    token_dest,
    token_row,
    prompt_text,
    kv_gain,
    w_kv,
    queries,
    resp_kv,
    resp_len,
):
    ctx_index = lax.axis_index("ctx")
    vis_index = lax.axis_index("vis")
    group = vis_index // 4

    local = patches.reshape(LOCAL // 4, 4, VD).transpose(1, 0, 2).reshape(LOCAL, VD)
    w_pad = jnp.pad(w_qkv.reshape(VD, 3, VHD), ((0, 0), (0, 0), (0, 128 - VHD))).reshape(VD, 384)
    owners = ring_owners(vis_index)

    patch_blocks = ring_gather(local)

    across = [(c * N + v, v * N + c) for c in range(N) for v in range(N)]
    out_block = lax.ppermute(w_out, ("ctx", "vis"), across)
    patch_blocks[1], patch_blocks[6], out_block = lax.optimization_barrier(
        (patch_blocks[1], patch_blocks[6], out_block)
    )
    own_q = lax.dynamic_slice_in_dim(queries, vis_index * 256, 256, 1)
    columns = [out_block[:, j * WIDE : j * WIDE + WIDE] for j in range(VD // WIDE)]
    shared = lax.all_gather(jnp.concatenate([own_q, *columns], axis=0), "ctx", axis=0)

    w_kv_mine = w_kv.reshape(512, 2, KVH, 2, 64).transpose(0, 2, 1, 3, 4).reshape(512, 1024)
    text = prompt_text.astype(f32)
    text_squares = jnp.sum(text * text, axis=1)
    text_gained = (text * kv_gain).astype(bf16)
    text_part = dot(w_kv_mine, text_gained, (0, 1)).reshape(N, 64, CROWS)
    text_extra = jnp.broadcast_to(text_squares[None, None, :], (N, 8, CROWS))
    text_part = jnp.concatenate([text_part, text_extra], axis=1).reshape(N * CHUNK, CROWS)

    flat_dest = token_dest.reshape(-1)
    flat_row = token_row.reshape(-1)
    here = jnp.where(flat_dest == ctx_index, flat_row // 128, -1)
    tall = (here[None, :] == jnp.arange(8, dtype=jnp.int32)[:, None]).astype(bf16)
    wide = ((flat_row % 128)[:, None] == jnp.arange(128, dtype=jnp.int32)[None, :]).astype(bf16)
    taken = dot(tall, wide, (1, 0)).reshape(1, CROWS)
    mask = jnp.where(taken > 0.5, NEG, 0.0)
    mask = jnp.concatenate([mask, jnp.zeros((1, VTOK), f32)], axis=1)

    own_k = lax.dynamic_slice_in_dim(resp_kv, group * HD, HD, 1)
    own_v = lax.dynamic_slice_in_dim(resp_kv, KVH * HD + group * HD, HD, 1)
    positions = jnp.arange(R_TOK, dtype=jnp.int32)
    visible = positions[None, :] <= positions[:, None]
    q_two = own_q.reshape(R_TOK, 2, HD)
    own_scores = jnp.einsum("rhd,nd->hrn", q_two, own_k, preferred_element_type=f32)
    own_scores = jnp.where(visible, own_scores * (1.0 / math.sqrt(HD)), NEG)
    own_high = jnp.max(own_scores, axis=2, keepdims=True)
    own_expo = jnp.where(visible, jnp.exp(own_scores - own_high), 0.0)
    own_total = jnp.sum(own_expo, axis=2, keepdims=True)
    own_mixed = jnp.einsum("hrn,nd->hrd", own_expo.astype(bf16), own_v, preferred_element_type=f32)
    own_mixed = (own_mixed / own_total).reshape(256, HD)
    own_level = (own_high * LOG2E + jnp.log2(own_total)).reshape(1, 256)

    patch_blocks[2], patch_blocks[7], text_part = lax.optimization_barrier(
        (patch_blocks[2], patch_blocks[7], text_part)
    )
    own_heads, image = vision(owners, patch_blocks, vis_gain.reshape(1, VD), w_pad)
    text_sum = lax.psum_scatter(text_part, "vis", scatter_dimension=0, tiled=True)
    text_scale = lax.rsqrt(text_sum[64:65] / D + EPS)
    text_kv = (text_sum[:64] * text_scale).astype(bf16)

    partial = merge(
        owners,
        ring_gather(own_heads),
        image,
        shared,
        merge_gain.reshape(1, VD),
        w_merge,
        kv_gain.reshape(1, 512),
        w_kv_mine,
    )
    arrived = lax.all_to_all(partial, "vis", split_axis=0, concat_axis=0, tiled=True)
    vis_sum = jnp.sum(arrived.astype(f32), axis=0)
    vis_squares = vis_sum[64:65] + vis_sum[65:66] + vis_sum[66:67]
    vis_kv = (vis_sum[:64] * lax.rsqrt(vis_squares / D + EPS)).astype(bf16)
    kv = jnp.concatenate([text_kv, vis_kv], axis=1)
    kv = lax.all_gather(kv, "vis", axis=0, tiled=True, axis_index_groups=QUADS)
    packed = response(shared, kv, mask)
    back = lax.all_to_all(packed, "ctx", split_axis=0, concat_axis=0, tiled=True).astype(f32)
    levels = back[:, 256:258] + back[:, 258:260] + back[:, 260:262]
    levels = levels.reshape(N, 256)
    highest = jnp.maximum(jnp.max(levels, axis=0, keepdims=True), own_level)
    weights = jnp.exp2(levels - highest)
    own_weight = jnp.exp2(own_level - highest)
    total = jnp.sum(weights, axis=0, keepdims=True) + own_weight
    weights = weights / total
    own_weight = own_weight / total
    result = jnp.sum(back[:, :256] * weights[:, :, None], axis=0)
    result = result + own_mixed * own_weight.reshape(256, 1)
    result = jnp.transpose(result.reshape(2, R_TOK, HD), (1, 0, 2)).reshape(R_TOK, 256)
    live = (positions < resp_len[0])[:, None]
    result = jnp.where(live, result, 0.0).astype(bf16)
    return placed(owners, ring_gather(result))


def solution(mesh):
    return jax.shard_map(
        per_device,
        mesh=mesh,
        in_specs=(
            P(("ctx", "vis"), None),
            P(),
            P(None, "vis"),
            P("vis", None),
            P(),
            P(None, "vis"),
            P(),
            P(),
            P("ctx", "vis"),
            P("vis"),
            P("vis", None),
            P("ctx", None),
            P("ctx", None),
            P("ctx"),
        ),
        out_specs=P("ctx", None),
        check_vma=False,
    )
```

```python
import math

import jax
import jax.numpy as jnp
from jax import lax
from jax.experimental import pallas as pl
from jax.experimental.pallas import tpu as pltpu
from jax.sharding import PartitionSpec as P

VD = 1280
VHEADS = 16
D = 8192
HD = 128
QH = 32
KVH = 4
CROWS = 1024
R_TOK = 128
VHD = 80
GP = 2048
VTOK = 512
N = 16
LOCAL = GP // N
EPS = 1e-06
NEG = -1e30
bf16 = jnp.bfloat16
f32 = jnp.float32

QUADS = [[4 * g + i for i in range(4)] for g in range(4)]
LOG2E = math.log2(math.e)


def onward(block):
    pairs = [(2 * z, 2 * ((z + 1) % 8)) for z in range(8)]
    pairs += [(2 * z + 1, 2 * ((z - 1) % 8) + 1) for z in range(8)]
    return lax.ppermute(block, "vis", pairs)


def swapped(block):
    return lax.ppermute(block, "vis", [(i, i ^ 1) for i in range(N)])


def ring_gather(block):
    same = [block]
    other = [swapped(block)]
    for step in range(3):
        same.append(onward(same[-1]))
        other.append(onward(other[-1]))
    same.append(onward(same[-1]))
    away = [swapped(piece) for piece in same[1:]]
    back = [swapped(piece) for piece in other[1:]]
    return same + other + away + back


def ring_owners(vis_index):
    z = vis_index // 2
    core = vis_index % 2
    sign = 2 * core - 1
    hops = jnp.array((0, 1, 2, 3, 4, 0, 1, 2, 3, -1, -2, -3, -4, -1, -2, -3), jnp.int32)
    flips = jnp.array((0,) * 5 + (1,) * 4 + (1,) * 4 + (0,) * 3, jnp.int32)
    return (z + sign * hops) % 8 * 2 + (core + flips) % 2


def dot(a, b, contract):
    return lax.dot_general(a, b, ((contract[:1], contract[1:]), ((), ())), preferred_element_type=f32)


def normed_rows(values, gain):
    center = values - jnp.mean(values, axis=-1, keepdims=True)
    spread = jnp.mean(center * center, axis=-1, keepdims=True)
    return center * lax.rsqrt(spread + EPS) * gain


QKV_STEPS = 4
QKV_ROWS = GP // QKV_STEPS
ATT_STEPS = 2
ATT_ROWS = GP // ATT_STEPS
ATT_PART = 256


def vision_kernel(x_ref, gain_ref, w_ref, out_ref, w_s, q_s, k_s, v_s):
    step = pl.program_id(0)

    @pl.when(step == 0)
    def _():
        for part in range(3):
            w_s[part * 128 : part * 128 + VHD, :] = w_ref[part * VHD : part * VHD + VHD, :]
            w_s[part * 128 + VHD : part * 128 + 128, :] = jnp.zeros((128 - VHD, VD), bf16)

    @pl.when(step < QKV_STEPS)
    def _():
        rows = x_ref[...].reshape(QKV_ROWS, VD)
        normed = normed_rows(rows.astype(f32), gain_ref[...]).astype(bf16)
        qkv = dot(normed, w_s[...], (1, 1)).astype(bf16)
        rows = pl.ds(pl.multiple_of(step * QKV_ROWS, QKV_ROWS), QKV_ROWS)
        q_s[rows, :] = qkv[:, :128]
        k_s[rows, :] = qkv[:, 128:256]
        lane = lax.broadcasted_iota(jnp.int32, (QKV_ROWS, 128), 1)
        v_s[rows, :] = jnp.where(lane == VHD, jnp.ones((), bf16), qkv[:, 256:])

    @pl.when(step >= QKV_STEPS)
    def _():
        first = pl.multiple_of((step - QKV_STEPS) * ATT_ROWS, ATT_ROWS)
        for part in range(0, ATT_ROWS, ATT_PART):
            query = q_s[pl.ds(first + part, ATT_PART), :]
            scores = dot(query, k_s[...], (1, 1))
            highest = jnp.max(scores, axis=1, keepdims=True)
            expo = jnp.exp2((scores - highest) * (LOG2E / math.sqrt(VHD))).astype(bf16)
            mixed = dot(expo, v_s[...], (1, 0))
            mixed = mixed / mixed[:, VHD : VHD + 1]
            out_ref[:, part : part + ATT_PART] = jnp.transpose(mixed, (1, 0))[:VHD, :].astype(bf16)


def vision(x, gain, w):
    return pl.pallas_call(
        vision_kernel,
        grid=(QKV_STEPS + ATT_STEPS,),
        in_specs=[
            pl.BlockSpec((N // QKV_STEPS, LOCAL, VD), lambda i: (jnp.minimum(i, QKV_STEPS - 1), 0, 0)),
            pl.BlockSpec((1, VD), lambda i: (0, 0)),
            pl.BlockSpec((3 * VHD, VD), lambda i: (0, 0)),
        ],
        out_specs=pl.BlockSpec((VHD, ATT_ROWS), lambda i: (0, jnp.maximum(i - QKV_STEPS, 0))),
        out_shape=jax.ShapeDtypeStruct((VHD, GP), bf16),
        scratch_shapes=[pltpu.VMEM((384, VD), bf16)] + [pltpu.VMEM((GP, 128), bf16)] * 3,
        compiler_params=pltpu.CompilerParams(vmem_limit_bytes=60 * 2**20),
        name="vision",
    )(x, gain, w)


MERGE_STEPS = 4
MERGE_ROWS = GP // MERGE_STEPS
MERGE_TOK = VTOK // MERGE_STEPS
CHUNK = 72
HELD = N


def row_of(column):
    count = column.shape[0]
    down = lax.broadcasted_iota(jnp.int32, (count, count), 0)
    across = lax.broadcasted_iota(jnp.int32, (count, count), 1)
    return jnp.sum(jnp.where(down == across, column, 0.0), axis=0, keepdims=True)


def three_parts(row):
    high = row.astype(bf16).astype(f32)
    middle = (row - high).astype(bf16).astype(f32)
    return high, middle, row - high - middle


def merge_kernel(order_ref, *refs):
    pieces = refs[:HELD]
    x_ref, all_ref, gain_ref, wm_ref, kg_ref, wk_ref, out_ref, heads_s, merged_s, wo_s, sems = refs[HELD:]
    step = pl.program_id(0)

    def fetch(k):
        source = all_ref.at[k, pl.ds(LOCAL, VHD), :]
        return pltpu.make_async_copy(source, wo_s.at[pl.ds(k * VHD, VHD), :], sems.at[k])

    @pl.when(step == 0)
    def _():
        for k in range(N):
            fetch(k).start()

    for k in range(N):
        first = pl.multiple_of(order_ref[k] * VHD, VHD)
        heads_s[pl.ds(first, VHD), :] = pieces[k][...]

    @pl.when(step == 0)
    def _():
        for k in range(N):
            fetch(k).wait()

    floats = x_ref[...].reshape(MERGE_ROWS, VD).astype(f32)
    mixed = floats + dot(heads_s[...], wo_s[...], (0, 0))
    merged = normed_rows(mixed, gain_ref[...]).astype(bf16)
    split = merged.reshape(MERGE_ROWS // LOCAL, 4, LOCAL // 4, VD)
    rows = pl.ds(pl.multiple_of(step * MERGE_TOK, MERGE_TOK), MERGE_TOK)
    for a in range(4):
        merged_s[rows, a * VD : (a + 1) * VD] = split[:, a].reshape(MERGE_TOK, VD)

    @pl.when(step == MERGE_STEPS - 1)
    def _():
        visual = dot(merged_s[...], wm_ref[...], (1, 0)).astype(bf16).astype(f32)
        squares = row_of(jnp.sum(visual * visual, axis=1, keepdims=True))
        zeros = jnp.zeros((CHUNK - 67, VTOK), f32)
        extra = jnp.concatenate([*three_parts(squares), zeros], axis=0)
        gained = (visual * kg_ref[...]).astype(bf16)
        kv = dot(wk_ref[...], gained, (1, 1))
        for v in range(N):
            both = jnp.concatenate([kv[64 * v : 64 * v + 64, :], extra], axis=0)
            out_ref[v, :, :] = both.astype(bf16)


def merge(order, pieces, x, gain, w_merge, kv_gain, w_kv):
    whole = lambda i, order: (0, 0)
    grid_spec = pltpu.PrefetchScalarGridSpec(
        num_scalar_prefetch=1,
        grid=(MERGE_STEPS,),
        in_specs=[
            pl.BlockSpec((piece.shape[0], MERGE_ROWS), lambda i, order: (0, i)) for piece in pieces
        ]
        + [
            pl.BlockSpec((N // MERGE_STEPS, LOCAL, VD), lambda i, order: (i, 0, 0)),
            pl.BlockSpec(memory_space=pl.ANY),
            pl.BlockSpec((1, VD), whole),
            pl.BlockSpec((4 * VD, 512), whole),
            pl.BlockSpec((1, 512), whole),
            pl.BlockSpec((1024, 512), whole),
        ],
        out_specs=pl.BlockSpec((N, CHUNK, VTOK), lambda i, order: (0, 0, 0)),
        scratch_shapes=[
            pltpu.VMEM((VD, MERGE_ROWS), bf16),
            pltpu.VMEM((VTOK, 4 * VD), bf16),
            pltpu.VMEM((VD, VD), bf16),
            pltpu.SemaphoreType.DMA((N,)),
        ],
    )
    return pl.pallas_call(
        merge_kernel,
        grid_spec=grid_spec,
        out_shape=jax.ShapeDtypeStruct((N, CHUNK, VTOK), bf16),
        compiler_params=pltpu.CompilerParams(vmem_limit_bytes=56 * 2**20),
        name="merge",
    )(order, *pieces, x, x, gain, w_merge, kv_gain, w_kv)


PACK = 272
PER = 8
SCALE2 = LOG2E / math.sqrt(HD)


def response_kernel(qa_ref, qb_ref, kv_ref, ones_ref, mask_ref, out_ref):
    values = jnp.concatenate([kv_ref[HD:, :], ones_ref[...]], axis=0)
    for r in range(PER):
        qa, qb = qa_ref[r], qb_ref[r]
        query = jnp.concatenate([qa[:, :HD], qb[:, :HD], qa[:, HD:], qb[:, HD:]], axis=0)
        scores = dot(query, kv_ref[:HD, :], (1, 0)) + mask_ref[...]
        highest = jnp.max(scores, axis=1, keepdims=True)
        expo = jnp.exp2((scores - highest) * SCALE2).astype(bf16)
        mixed = dot(expo, values, (1, 1))
        total = mixed[:, HD : HD + 1]
        out_ref[r, : 2 * R_TOK, :] = (mixed[:, :HD] / total).astype(bf16)
        level = row_of(highest * SCALE2 + jnp.log2(total))
        parts = [part[:, k * HD : k * HD + HD] for part in three_parts(level) for k in range(2)]
        tail = jnp.concatenate(parts + [jnp.zeros((10, HD), f32)], axis=0)
        out_ref[r, 2 * R_TOK :, :] = tail.astype(bf16)


def response(qa, qb, kv, mask):
    whole = lambda i: (0, 0)
    some = lambda i: (i, 0, 0)
    keys = CROWS + VTOK
    return pl.pallas_call(
        response_kernel,
        grid=(N // PER,),
        in_specs=[
            pl.BlockSpec((PER, R_TOK // 2, 2 * HD), some),
            pl.BlockSpec((PER, R_TOK // 2, 2 * HD), some),
            pl.BlockSpec((2 * HD, keys), whole),
            pl.BlockSpec((HD, keys), whole),
            pl.BlockSpec((1, keys), whole),
        ],
        out_specs=pl.BlockSpec((PER, PACK, HD), some),
        out_shape=jax.ShapeDtypeStruct((N, PACK, HD), bf16),
        compiler_params=pltpu.CompilerParams(vmem_limit_bytes=48 * 2**20),
        name="response",
    )(qa, qb, kv, jnp.ones((HD, keys), bf16), mask)


def place_kernel(order_ref, *refs):
    out_ref = refs[-1]
    for k in range(N):
        first = pl.multiple_of(order_ref[k] * 2 * HD, 2 * HD)
        out_ref[:, pl.ds(first, 2 * HD)] = refs[k][...]


def placed(order, pieces):
    whole = lambda i, order: (0, 0)
    grid_spec = pltpu.PrefetchScalarGridSpec(
        num_scalar_prefetch=1,
        grid=(1,),
        in_specs=[pl.BlockSpec((R_TOK, 2 * HD), whole)] * N,
        out_specs=pl.BlockSpec((R_TOK, QH * HD), whole),
    )
    return pl.pallas_call(
        place_kernel,
        grid_spec=grid_spec,
        out_shape=jax.ShapeDtypeStruct((R_TOK, QH * HD), bf16),
        name="placed",
    )(order, *pieces)


def per_device(
    patches,
    vis_gain,
    w_qkv,
    w_out,
    merge_gain,
    w_merge,
    token_dest,
    token_row,
    prompt_text,
    kv_gain,
    w_kv,
    queries,
    resp_kv,
    resp_len,
):
    ctx_index = lax.axis_index("ctx")
    vis_index = lax.axis_index("vis")
    group = vis_index // 4

    local = patches.reshape(LOCAL // 4, 4, VD).transpose(1, 0, 2).reshape(LOCAL, VD)
    image = lax.all_gather(jnp.concatenate([local, w_out], axis=0), "vis", axis=0)
    w_turned = jnp.transpose(w_qkv, (1, 0))

    w_kv_mine = w_kv.T.reshape(2, KVH, 2, 64, 512).transpose(1, 0, 2, 3, 4).reshape(1024, 512)
    text = prompt_text.astype(f32)
    text_squares = jnp.sum(text * text, axis=1)
    text_gained = (text * kv_gain).astype(bf16)
    text_part = dot(w_kv_mine, text_gained, (1, 1)).reshape(N, 64, CROWS)
    text_extra = jnp.broadcast_to(text_squares[None, None, :], (N, 8, CROWS))
    text_part = jnp.concatenate([text_part, text_extra], axis=1).reshape(N * CHUNK, CROWS)

    own_q = lax.dynamic_slice_in_dim(queries, vis_index * 256, 256, 1)
    own_q, text_part = lax.optimization_barrier((own_q, text_part))
    half = R_TOK // 2
    qa = lax.all_gather(own_q[:half], "ctx", axis=0)
    qb = lax.all_gather(own_q[half:], "ctx", axis=0)

    flat_dest = token_dest.reshape(-1)
    flat_row = token_row.reshape(-1)
    here = jnp.where(flat_dest == ctx_index, flat_row // 128, -1)
    tall = (here[None, :] == jnp.arange(8, dtype=jnp.int32)[:, None]).astype(bf16)
    wide = ((flat_row % 128)[:, None] == jnp.arange(128, dtype=jnp.int32)[None, :]).astype(bf16)
    taken = dot(tall, wide, (1, 0)).reshape(1, CROWS)
    mask = jnp.where(taken > 0.5, NEG, 0.0)
    mask = jnp.concatenate([mask, jnp.zeros((1, VTOK), f32)], axis=1)

    own_k = lax.dynamic_slice_in_dim(resp_kv, group * HD, HD, 1)
    own_v = lax.dynamic_slice_in_dim(resp_kv, KVH * HD + group * HD, HD, 1)
    positions = jnp.arange(R_TOK, dtype=jnp.int32)
    visible = positions[None, :] <= positions[:, None]
    q_two = own_q.reshape(R_TOK, 2, HD)
    own_scores = jnp.einsum("rhd,nd->hrn", q_two, own_k, preferred_element_type=f32)
    own_scores = jnp.where(visible, own_scores * (1.0 / math.sqrt(HD)), NEG)
    own_high = jnp.max(own_scores, axis=2, keepdims=True)
    own_expo = jnp.where(visible, jnp.exp(own_scores - own_high), 0.0)
    own_total = jnp.sum(own_expo, axis=2, keepdims=True)
    own_mixed = jnp.einsum("hrn,nd->hrd", own_expo.astype(bf16), own_v, preferred_element_type=f32)
    own_mixed = (own_mixed / own_total).reshape(256, HD)
    own_level = (own_high * LOG2E + jnp.log2(own_total)).reshape(1, 256)

    image, qa, qb, text_part = lax.optimization_barrier((image, qa, qb, text_part))
    own_heads = vision(image, vis_gain.reshape(1, VD), w_turned)
    text_sum = lax.psum_scatter(text_part, "vis", scatter_dimension=0, tiled=True)
    text_scale = lax.rsqrt(text_sum[64:65] / D + EPS)
    text_kv = (text_sum[:64] * text_scale).astype(bf16)
    owners = ring_owners(vis_index)
    partial = merge(
        owners,
        ring_gather(own_heads),
        image,
        merge_gain.reshape(1, VD),
        w_merge,
        kv_gain.reshape(1, 512),
        w_kv_mine,
    )
    arrived = lax.all_to_all(partial, "vis", split_axis=0, concat_axis=0, tiled=True)
    arrived, text_kv = lax.optimization_barrier((arrived, text_kv))
    vis_sum = jnp.sum(arrived.astype(f32), axis=0)
    vis_squares = vis_sum[64:65] + vis_sum[65:66] + vis_sum[66:67]
    vis_kv = (vis_sum[:64] * lax.rsqrt(vis_squares / D + EPS)).astype(bf16)
    kv = jnp.concatenate([text_kv, vis_kv], axis=1)
    kv = lax.all_gather(kv, "vis", axis=0, tiled=True, axis_index_groups=QUADS)
    packed = response(qa, qb, kv, mask)
    back = lax.all_to_all(packed, "ctx", split_axis=0, concat_axis=0, tiled=True).astype(f32)
    levels = back[:, 256:258] + back[:, 258:260] + back[:, 260:262]
    levels = levels.reshape(N, 256)
    highest = jnp.maximum(jnp.max(levels, axis=0, keepdims=True), own_level)
    weights = jnp.exp2(levels - highest)
    own_weight = jnp.exp2(own_level - highest)
    total = jnp.sum(weights, axis=0, keepdims=True) + own_weight
    weights = weights / total
    own_weight = own_weight / total
    result = jnp.sum(back[:, :256] * weights[:, :, None], axis=0)
    result = result + own_mixed * own_weight.reshape(256, 1)
    result = jnp.transpose(result.reshape(2, R_TOK, HD), (1, 0, 2)).reshape(R_TOK, 256)
    live = (positions < resp_len[0])[:, None]
    result = jnp.where(live, result, 0.0).astype(bf16)
    return placed(owners, ring_gather(result))


def solution(mesh):
    return jax.shard_map(
        per_device,
        mesh=mesh,
        in_specs=(
            P(("ctx", "vis"), None),
            P(),
            P(None, "vis"),
            P("vis", None),
            P(),
            P(None, "vis"),
            P(),
            P(),
            P("ctx", "vis"),
            P("vis"),
            P("vis", None),
            P("ctx", None),
            P("ctx", None),
            P("ctx"),
        ),
        out_specs=P("ctx", None),
        check_vma=False,
    )
```

```python
import math

import jax
import jax.numpy as jnp
from jax import lax
from jax.experimental import pallas as pl
from jax.experimental.pallas import tpu as pltpu
from jax.sharding import PartitionSpec as P

VD = 1280
VHEADS = 16
D = 8192
HD = 128
QH = 32
KVH = 4
CROWS = 1024
R_TOK = 128
VHD = 80
GP = 2048
VTOK = 512
N = 16
LOCAL = GP // N
EPS = 1e-06
NEG = -1e30
bf16 = jnp.bfloat16
f32 = jnp.float32

QUADS = [[4 * g + i for i in range(4)] for g in range(4)]
LOG2E = math.log2(math.e)


def onward(block):
    pairs = [(2 * z, 2 * ((z + 1) % 8)) for z in range(8)]
    pairs += [(2 * z + 1, 2 * ((z - 1) % 8) + 1) for z in range(8)]
    return lax.ppermute(block, "vis", pairs)


def swapped(block):
    return lax.ppermute(block, "vis", [(i, i ^ 1) for i in range(N)])


def ring_gather(block):
    same = [block]
    other = [swapped(block)]
    for step in range(3):
        same.append(onward(same[-1]))
        other.append(onward(other[-1]))
    same.append(onward(same[-1]))
    away = [swapped(piece) for piece in same[1:]]
    back = [swapped(piece) for piece in other[1:]]
    return same + other + away + back


def ring_owners(vis_index):
    z = vis_index // 2
    core = vis_index % 2
    sign = 2 * core - 1
    hops = jnp.array((0, 1, 2, 3, 4, 0, 1, 2, 3, -1, -2, -3, -4, -1, -2, -3), jnp.int32)
    flips = jnp.array((0,) * 5 + (1,) * 4 + (1,) * 4 + (0,) * 3, jnp.int32)
    return (z + sign * hops) % 8 * 2 + (core + flips) % 2


def dot(a, b, contract):
    return lax.dot_general(a, b, ((contract[:1], contract[1:]), ((), ())), preferred_element_type=f32)


def normed_rows(values, gain):
    center = values - jnp.mean(values, axis=-1, keepdims=True)
    spread = jnp.mean(center * center, axis=-1, keepdims=True)
    return center * lax.rsqrt(spread + EPS) * gain


QKV_STEPS = 4
QKV_ROWS = GP // QKV_STEPS
ATT_STEPS = 2
ATT_ROWS = GP // ATT_STEPS
ATT_PART = 256


def vision_kernel(x_ref, gain_ref, w_ref, out_ref, w_s, q_s, k_s, v_s):
    step = pl.program_id(0)

    @pl.when(step == 0)
    def _():
        for part in range(3):
            w_s[part * 128 : part * 128 + VHD, :] = w_ref[part * VHD : part * VHD + VHD, :]
            w_s[part * 128 + VHD : part * 128 + 128, :] = jnp.zeros((128 - VHD, VD), bf16)

    @pl.when(step < QKV_STEPS)
    def _():
        rows = x_ref[...].reshape(QKV_ROWS, VD)
        normed = normed_rows(rows.astype(f32), gain_ref[...]).astype(bf16)
        qkv = dot(normed, w_s[...], (1, 1)).astype(bf16)
        rows = pl.ds(pl.multiple_of(step * QKV_ROWS, QKV_ROWS), QKV_ROWS)
        q_s[rows, :] = qkv[:, :128]
        k_s[rows, :] = qkv[:, 128:256]
        lane = lax.broadcasted_iota(jnp.int32, (QKV_ROWS, 128), 1)
        v_s[rows, :] = jnp.where(lane == VHD, jnp.ones((), bf16), qkv[:, 256:])

    @pl.when(step >= QKV_STEPS)
    def _():
        first = pl.multiple_of((step - QKV_STEPS) * ATT_ROWS, ATT_ROWS)
        for part in range(0, ATT_ROWS, ATT_PART):
            query = q_s[pl.ds(first + part, ATT_PART), :]
            scores = dot(query, k_s[...], (1, 1))
            highest = jnp.max(scores, axis=1, keepdims=True)
            expo = jnp.exp2((scores - highest) * (LOG2E / math.sqrt(VHD))).astype(bf16)
            mixed = dot(expo, v_s[...], (1, 0))
            mixed = mixed / mixed[:, VHD : VHD + 1]
            out_ref[:, part : part + ATT_PART] = jnp.transpose(mixed, (1, 0))[:VHD, :].astype(bf16)


def vision(x, gain, w):
    return pl.pallas_call(
        vision_kernel,
        grid=(QKV_STEPS + ATT_STEPS,),
        in_specs=[
            pl.BlockSpec((N // QKV_STEPS, LOCAL, VD), lambda i: (jnp.minimum(i, QKV_STEPS - 1), 0, 0)),
            pl.BlockSpec((1, VD), lambda i: (0, 0)),
            pl.BlockSpec((3 * VHD, VD), lambda i: (0, 0)),
        ],
        out_specs=pl.BlockSpec((VHD, ATT_ROWS), lambda i: (0, jnp.maximum(i - QKV_STEPS, 0))),
        out_shape=jax.ShapeDtypeStruct((VHD, GP), bf16),
        scratch_shapes=[pltpu.VMEM((384, VD), bf16)] + [pltpu.VMEM((GP, 128), bf16)] * 3,
        compiler_params=pltpu.CompilerParams(vmem_limit_bytes=60 * 2**20),
        name="vision",
    )(x, gain, w)


MERGE_STEPS = 4
MERGE_ROWS = GP // MERGE_STEPS
MERGE_TOK = VTOK // MERGE_STEPS
CHUNK = 72
HELD = N
WIDE = 256


def row_of(column):
    count = column.shape[0]
    down = lax.broadcasted_iota(jnp.int32, (count, count), 0)
    across = lax.broadcasted_iota(jnp.int32, (count, count), 1)
    return jnp.sum(jnp.where(down == across, column, 0.0), axis=0, keepdims=True)


def three_parts(row):
    high = row.astype(bf16).astype(f32)
    middle = (row - high).astype(bf16).astype(f32)
    return high, middle, row - high - middle


def merge_kernel(order_ref, *refs):
    pieces = refs[:HELD]
    x_ref, all_ref, gain_ref, wm_ref, kg_ref, wk_ref, out_ref = refs[HELD : HELD + 7]
    heads_s, merged_s, wo_s, wm_s, sems, wm_sem = refs[HELD + 7 :]
    step = pl.program_id(0)

    def fetch(k, j):
        source = all_ref.at[k, pl.ds(R_TOK + j * VHD, VHD), :]
        target = wo_s.at[pl.ds(k * VHD, VHD), pl.ds(j * WIDE, WIDE)]
        return pltpu.make_async_copy(source, target, sems.at[k, j])

    weights = pltpu.make_async_copy(wm_ref, wm_s, wm_sem)

    @pl.when(step == 0)
    def _():
        for k in range(N):
            for j in range(VD // WIDE):
                fetch(k, j).start()
        weights.start()

    for k in range(N):
        first = pl.multiple_of(order_ref[k] * VHD, VHD)
        heads_s[pl.ds(first, VHD), :] = pieces[k][...]

    @pl.when(step == 0)
    def _():
        for k in range(N):
            for j in range(VD // WIDE):
                fetch(k, j).wait()

    floats = x_ref[...].reshape(MERGE_ROWS, VD).astype(f32)
    mixed = floats + dot(heads_s[...], wo_s[...], (0, 0))
    merged = normed_rows(mixed, gain_ref[...]).astype(bf16)
    split = merged.reshape(MERGE_ROWS // LOCAL, 4, LOCAL // 4, VD)
    rows = pl.ds(pl.multiple_of(step * MERGE_TOK, MERGE_TOK), MERGE_TOK)
    for a in range(4):
        merged_s[rows, a * VD : (a + 1) * VD] = split[:, a].reshape(MERGE_TOK, VD)

    @pl.when(step == MERGE_STEPS - 1)
    def _():
        weights.wait()
        visual = dot(merged_s[...], wm_s[...], (1, 0)).astype(bf16).astype(f32)
        squares = row_of(jnp.sum(visual * visual, axis=1, keepdims=True))
        zeros = jnp.zeros((CHUNK - 67, VTOK), f32)
        extra = jnp.concatenate([*three_parts(squares), zeros], axis=0)
        gained = (visual * kg_ref[...]).astype(bf16)
        kv = dot(wk_ref[...], gained, (1, 1))
        for v in range(N):
            both = jnp.concatenate([kv[64 * v : 64 * v + 64, :], extra], axis=0)
            out_ref[v, :, :] = both.astype(bf16)


def merge(order, pieces, x, shared, gain, w_merge, kv_gain, w_kv):
    whole = lambda i, order: (0, 0)
    grid_spec = pltpu.PrefetchScalarGridSpec(
        num_scalar_prefetch=1,
        grid=(MERGE_STEPS,),
        in_specs=[
            pl.BlockSpec((piece.shape[0], MERGE_ROWS), lambda i, order: (0, i)) for piece in pieces
        ]
        + [
            pl.BlockSpec((N // MERGE_STEPS, LOCAL, VD), lambda i, order: (i, 0, 0)),
            pl.BlockSpec(memory_space=pl.ANY),
            pl.BlockSpec((1, VD), whole),
            pl.BlockSpec(memory_space=pl.ANY),
            pl.BlockSpec((1, 512), whole),
            pl.BlockSpec((1024, 512), whole),
        ],
        out_specs=pl.BlockSpec((N, CHUNK, VTOK), lambda i, order: (0, 0, 0)),
        scratch_shapes=[
            pltpu.VMEM((VD, MERGE_ROWS), bf16),
            pltpu.VMEM((VTOK, 4 * VD), bf16),
            pltpu.VMEM((VD, VD), bf16),
            pltpu.VMEM((4 * VD, 512), bf16),
            pltpu.SemaphoreType.DMA((N, VD // WIDE)),
            pltpu.SemaphoreType.DMA,
        ],
    )
    return pl.pallas_call(
        merge_kernel,
        grid_spec=grid_spec,
        out_shape=jax.ShapeDtypeStruct((N, CHUNK, VTOK), bf16),
        compiler_params=pltpu.CompilerParams(vmem_limit_bytes=56 * 2**20),
        name="merge",
    )(order, *pieces, x, shared, gain, w_merge, kv_gain, w_kv)


PACK = 272
PER = 8
SCALE2 = LOG2E / math.sqrt(HD)


def response_kernel(q_ref, kv_ref, ones_ref, mask_ref, out_ref):
    values = jnp.concatenate([kv_ref[HD:, :], ones_ref[...]], axis=0)
    for r in range(PER):
        query = jnp.concatenate([q_ref[r, :, :HD], q_ref[r, :, HD:]], axis=0)
        scores = dot(query, kv_ref[:HD, :], (1, 0)) + mask_ref[...]
        highest = jnp.max(scores, axis=1, keepdims=True)
        expo = jnp.exp2((scores - highest) * SCALE2).astype(bf16)
        mixed = dot(expo, values, (1, 1))
        total = mixed[:, HD : HD + 1]
        out_ref[r, : 2 * R_TOK, :] = (mixed[:, :HD] / total).astype(bf16)
        level = row_of(highest * SCALE2 + jnp.log2(total))
        parts = [part[:, k * HD : k * HD + HD] for part in three_parts(level) for k in range(2)]
        tail = jnp.concatenate(parts + [jnp.zeros((10, HD), f32)], axis=0)
        out_ref[r, 2 * R_TOK :, :] = tail.astype(bf16)


def response(shared, kv, mask):
    whole = lambda i: (0, 0)
    some = lambda i: (i, 0, 0)
    keys = CROWS + VTOK
    return pl.pallas_call(
        response_kernel,
        grid=(N // PER,),
        in_specs=[
            pl.BlockSpec((PER, R_TOK, 2 * HD), some),
            pl.BlockSpec((2 * HD, keys), whole),
            pl.BlockSpec((HD, keys), whole),
            pl.BlockSpec((1, keys), whole),
        ],
        out_specs=pl.BlockSpec((PER, PACK, HD), some),
        out_shape=jax.ShapeDtypeStruct((N, PACK, HD), bf16),
        compiler_params=pltpu.CompilerParams(vmem_limit_bytes=48 * 2**20),
        name="response",
    )(shared, kv, jnp.ones((HD, keys), bf16), mask)


def place_kernel(order_ref, *refs):
    out_ref, sems = refs[N:]
    copies = []
    for k in range(N):
        first = pl.multiple_of(order_ref[k] * 2 * HD, 2 * HD)
        target = out_ref.at[:, pl.ds(first, 2 * HD)]
        copies.append(pltpu.make_async_copy(refs[k], target, sems.at[k]))
    for copy in copies:
        copy.start()
    for copy in copies:
        copy.wait()


def placed(order, pieces):
    grid_spec = pltpu.PrefetchScalarGridSpec(
        num_scalar_prefetch=1,
        grid=(1,),
        in_specs=[pl.BlockSpec(memory_space=pl.ANY)] * N,
        out_specs=pl.BlockSpec(memory_space=pl.ANY),
        scratch_shapes=[pltpu.SemaphoreType.DMA((N,))],
    )
    return pl.pallas_call(
        place_kernel,
        grid_spec=grid_spec,
        out_shape=jax.ShapeDtypeStruct((R_TOK, QH * HD), bf16),
        name="placed",
    )(order, *pieces)


def per_device(
    patches,
    vis_gain,
    w_qkv,
    w_out,
    merge_gain,
    w_merge,
    token_dest,
    token_row,
    prompt_text,
    kv_gain,
    w_kv,
    queries,
    resp_kv,
    resp_len,
):
    ctx_index = lax.axis_index("ctx")
    vis_index = lax.axis_index("vis")
    group = vis_index // 4

    local = patches.reshape(LOCAL // 4, 4, VD).transpose(1, 0, 2).reshape(LOCAL, VD)
    image = lax.all_gather(local, "vis", axis=0)
    w_turned = jnp.transpose(w_qkv, (1, 0))

    w_kv_mine = w_kv.T.reshape(2, KVH, 2, 64, 512).transpose(1, 0, 2, 3, 4).reshape(1024, 512)
    text = prompt_text.astype(f32)
    text_squares = jnp.sum(text * text, axis=1)
    text_gained = (text * kv_gain).astype(bf16)
    text_part = dot(w_kv_mine, text_gained, (1, 1)).reshape(N, 64, CROWS)
    text_extra = jnp.broadcast_to(text_squares[None, None, :], (N, 8, CROWS))
    text_part = jnp.concatenate([text_part, text_extra], axis=1).reshape(N * CHUNK, CROWS)

    own_q = lax.dynamic_slice_in_dim(queries, vis_index * 256, 256, 1)

    across = [(c * N + v, v * N + c) for c in range(N) for v in range(N)]
    out_block = lax.ppermute(w_out, ("ctx", "vis"), across)
    columns = [out_block[:, j * WIDE : j * WIDE + WIDE] for j in range(VD // WIDE)]
    payload = jnp.concatenate([own_q, *columns], axis=0)
    image, payload, text_part = lax.optimization_barrier((image, payload, text_part))
    shared = lax.all_gather(payload, "ctx", axis=0)

    flat_dest = token_dest.reshape(-1)
    flat_row = token_row.reshape(-1)
    here = jnp.where(flat_dest == ctx_index, flat_row // 128, -1)
    tall = (here[None, :] == jnp.arange(8, dtype=jnp.int32)[:, None]).astype(bf16)
    wide = ((flat_row % 128)[:, None] == jnp.arange(128, dtype=jnp.int32)[None, :]).astype(bf16)
    taken = dot(tall, wide, (1, 0)).reshape(1, CROWS)
    mask = jnp.where(taken > 0.5, NEG, 0.0)
    mask = jnp.concatenate([mask, jnp.zeros((1, VTOK), f32)], axis=1)

    own_k = lax.dynamic_slice_in_dim(resp_kv, group * HD, HD, 1)
    own_v = lax.dynamic_slice_in_dim(resp_kv, KVH * HD + group * HD, HD, 1)
    positions = jnp.arange(R_TOK, dtype=jnp.int32)
    visible = positions[None, :] <= positions[:, None]
    q_two = own_q.reshape(R_TOK, 2, HD)
    own_scores = jnp.einsum("rhd,nd->hrn", q_two, own_k, preferred_element_type=f32)
    own_scores = jnp.where(visible, own_scores * (1.0 / math.sqrt(HD)), NEG)
    own_high = jnp.max(own_scores, axis=2, keepdims=True)
    own_expo = jnp.where(visible, jnp.exp(own_scores - own_high), 0.0)
    own_total = jnp.sum(own_expo, axis=2, keepdims=True)
    own_mixed = jnp.einsum("hrn,nd->hrd", own_expo.astype(bf16), own_v, preferred_element_type=f32)
    own_mixed = (own_mixed / own_total).reshape(256, HD)
    own_level = (own_high * LOG2E + jnp.log2(own_total)).reshape(1, 256)

    head_blocks = ring_gather(vision(image, vis_gain.reshape(1, VD), w_turned))
    head_blocks[2], head_blocks[7], text_part = lax.optimization_barrier(
        (head_blocks[2], head_blocks[7], text_part)
    )
    text_sum = lax.psum_scatter(text_part, "vis", scatter_dimension=0, tiled=True)
    text_scale = lax.rsqrt(text_sum[64:65] / D + EPS)
    text_kv = (text_sum[:64] * text_scale).astype(bf16)
    owners = ring_owners(vis_index)
    partial = merge(
        owners,
        head_blocks,
        image,
        shared,
        merge_gain.reshape(1, VD),
        w_merge,
        kv_gain.reshape(1, 512),
        w_kv_mine,
    )
    arrived = lax.all_to_all(partial, "vis", split_axis=0, concat_axis=0, tiled=True)
    arrived, text_kv = lax.optimization_barrier((arrived, text_kv))
    vis_sum = jnp.sum(arrived.astype(f32), axis=0)
    vis_squares = vis_sum[64:65] + vis_sum[65:66] + vis_sum[66:67]
    vis_kv = (vis_sum[:64] * lax.rsqrt(vis_squares / D + EPS)).astype(bf16)
    kv = jnp.concatenate([text_kv, vis_kv], axis=1)
    kv = lax.all_gather(kv, "vis", axis=0, tiled=True, axis_index_groups=QUADS)
    packed = response(shared, kv, mask)
    back = lax.all_to_all(packed, "ctx", split_axis=0, concat_axis=0, tiled=True).astype(f32)
    levels = back[:, 256:258] + back[:, 258:260] + back[:, 260:262]
    levels = levels.reshape(N, 256)
    highest = jnp.maximum(jnp.max(levels, axis=0, keepdims=True), own_level)
    weights = jnp.exp2(levels - highest)
    own_weight = jnp.exp2(own_level - highest)
    total = jnp.sum(weights, axis=0, keepdims=True) + own_weight
    weights = weights / total
    own_weight = own_weight / total
    result = jnp.sum(back[:, :256] * weights[:, :, None], axis=0)
    result = result + own_mixed * own_weight.reshape(256, 1)
    result = jnp.transpose(result.reshape(2, R_TOK, HD), (1, 0, 2)).reshape(R_TOK, 256)
    live = (positions < resp_len[0])[:, None]
    result = jnp.where(live, result, 0.0).astype(bf16)
    return placed(owners, ring_gather(result))


def solution(mesh):
    return jax.shard_map(
        per_device,
        mesh=mesh,
        in_specs=(
            P(("ctx", "vis"), None),
            P(),
            P(None, "vis"),
            P("vis", None),
            P(),
            P(None, "vis"),
            P(),
            P(),
            P("ctx", "vis"),
            P("vis"),
            P("vis", None),
            P("ctx", None),
            P("ctx", None),
            P("ctx"),
        ),
        out_specs=P("ctx", None),
        check_vma=False,
    )
```

```python
import math

import jax
import jax.numpy as jnp
from jax import lax
from jax.experimental import pallas as pl
from jax.experimental.pallas import tpu as pltpu
from jax.sharding import PartitionSpec as P

VD = 1280
VHEADS = 16
D = 8192
HD = 128
QH = 32
KVH = 4
CROWS = 1024
R_TOK = 128
VHD = 80
GP = 2048
VTOK = 512
N = 16
LOCAL = GP // N
EPS = 1e-06
NEG = -1e30
bf16 = jnp.bfloat16
f32 = jnp.float32

QUADS = [[4 * g + i for i in range(4)] for g in range(4)]
LOG2E = math.log2(math.e)


def onward(block, hops=1):
    pairs = [(2 * z, 2 * ((z + hops) % 8)) for z in range(8)]
    pairs += [(2 * z + 1, 2 * ((z - hops) % 8) + 1) for z in range(8)]
    return lax.ppermute(block, "vis", pairs)


def swapped(block):
    return lax.ppermute(block, "vis", [(i, i ^ 1) for i in range(N)])


def ring_gather(block):
    same = [block]
    other = [swapped(block)]
    for step in range(3):
        same.append(onward(same[-1]))
        other.append(onward(other[-1]))
    same.append(onward(same[-1]))
    away = [swapped(piece) for piece in same[1:]]
    back = [swapped(piece) for piece in other[1:]]
    return same + other + away + back


def short_gather(block):
    same = [block, onward(block), onward(block, 2)]
    first = swapped(block)
    other = [first, onward(first), onward(first, 2)]
    same += [onward(same[1], 2), onward(same[2], 2)]
    other += [onward(other[1], 2)]
    away = [swapped(piece) for piece in same[1:]]
    back = [swapped(piece) for piece in other[1:]]
    return same + other + away + back


def ring_owners(vis_index):
    z = vis_index // 2
    core = vis_index % 2
    sign = 2 * core - 1
    hops = jnp.array((0, 1, 2, 3, 4, 0, 1, 2, 3, -1, -2, -3, -4, -1, -2, -3), jnp.int32)
    flips = jnp.array((0,) * 5 + (1,) * 4 + (1,) * 4 + (0,) * 3, jnp.int32)
    return (z + sign * hops) % 8 * 2 + (core + flips) % 2


def dot(a, b, contract):
    return lax.dot_general(a, b, ((contract[:1], contract[1:]), ((), ())), preferred_element_type=f32)


def normed_rows(values, gain):
    center = values - jnp.mean(values, axis=-1, keepdims=True)
    spread = jnp.mean(center * center, axis=-1, keepdims=True)
    return center * lax.rsqrt(spread + EPS) * gain


QKV_STEPS = 4
QKV_ROWS = GP // QKV_STEPS
ATT_STEPS = 2
ATT_ROWS = GP // ATT_STEPS
ATT_PART = 256


def vision_kernel(x_ref, gain_ref, w_ref, out_ref, w_s, q_s, k_s, v_s):
    step = pl.program_id(0)

    @pl.when(step == 0)
    def _():
        for part in range(3):
            w_s[part * 128 : part * 128 + VHD, :] = w_ref[part * VHD : part * VHD + VHD, :]
            w_s[part * 128 + VHD : part * 128 + 128, :] = jnp.zeros((128 - VHD, VD), bf16)

    @pl.when(step < QKV_STEPS)
    def _():
        rows = x_ref[...].reshape(QKV_ROWS, VD)
        normed = normed_rows(rows.astype(f32), gain_ref[...]).astype(bf16)
        qkv = dot(normed, w_s[...], (1, 1)).astype(bf16)
        rows = pl.ds(pl.multiple_of(step * QKV_ROWS, QKV_ROWS), QKV_ROWS)
        q_s[rows, :] = qkv[:, :128]
        k_s[rows, :] = qkv[:, 128:256]
        lane = lax.broadcasted_iota(jnp.int32, (QKV_ROWS, 128), 1)
        v_s[rows, :] = jnp.where(lane == VHD, jnp.ones((), bf16), qkv[:, 256:])

    @pl.when(step >= QKV_STEPS)
    def _():
        first = pl.multiple_of((step - QKV_STEPS) * ATT_ROWS, ATT_ROWS)
        for part in range(0, ATT_ROWS, ATT_PART):
            query = q_s[pl.ds(first + part, ATT_PART), :]
            scores = dot(query, k_s[...], (1, 1))
            highest = jnp.max(scores, axis=1, keepdims=True)
            expo = jnp.exp2((scores - highest) * (LOG2E / math.sqrt(VHD))).astype(bf16)
            mixed = dot(expo, v_s[...], (1, 0))
            mixed = mixed / mixed[:, VHD : VHD + 1]
            out_ref[:, part : part + ATT_PART] = jnp.transpose(mixed, (1, 0))[:VHD, :].astype(bf16)


def vision(x, gain, w):
    return pl.pallas_call(
        vision_kernel,
        grid=(QKV_STEPS + ATT_STEPS,),
        in_specs=[
            pl.BlockSpec((N // QKV_STEPS, LOCAL, VD), lambda i: (jnp.minimum(i, QKV_STEPS - 1), 0, 0)),
            pl.BlockSpec((1, VD), lambda i: (0, 0)),
            pl.BlockSpec((3 * VHD, VD), lambda i: (0, 0)),
        ],
        out_specs=pl.BlockSpec((VHD, ATT_ROWS), lambda i: (0, jnp.maximum(i - QKV_STEPS, 0))),
        out_shape=jax.ShapeDtypeStruct((VHD, GP), bf16),
        scratch_shapes=[pltpu.VMEM((384, VD), bf16)] + [pltpu.VMEM((GP, 128), bf16)] * 3,
        compiler_params=pltpu.CompilerParams(vmem_limit_bytes=60 * 2**20),
        name="vision",
    )(x, gain, w)


MERGE_STEPS = 4
MERGE_ROWS = GP // MERGE_STEPS
MERGE_TOK = VTOK // MERGE_STEPS
CHUNK = 72
HELD = N


def row_of(column):
    count = column.shape[0]
    down = lax.broadcasted_iota(jnp.int32, (count, count), 0)
    across = lax.broadcasted_iota(jnp.int32, (count, count), 1)
    return jnp.sum(jnp.where(down == across, column, 0.0), axis=0, keepdims=True)


def three_parts(row):
    high = row.astype(bf16).astype(f32)
    middle = (row - high).astype(bf16).astype(f32)
    return high, middle, row - high - middle


def merge_kernel(order_ref, *refs):
    pieces = refs[:HELD]
    x_ref, all_ref, gain_ref, wm_ref, kg_ref, wk_ref, out_ref = refs[HELD : HELD + 7]
    heads_s, merged_s, wo_s, wm_s, sems, wm_sem = refs[HELD + 7 :]
    step = pl.program_id(0)

    def fetch(k):
        source = all_ref.at[k, pl.ds(LOCAL, VHD), :]
        return pltpu.make_async_copy(source, wo_s.at[pl.ds(k * VHD, VHD), :], sems.at[k])

    weights = pltpu.make_async_copy(wm_ref, wm_s, wm_sem)

    @pl.when(step == 0)
    def _():
        for k in range(N):
            fetch(k).start()
        weights.start()

    for k in range(N):
        first = pl.multiple_of(order_ref[k] * VHD, VHD)
        heads_s[pl.ds(first, VHD), :] = pieces[k][...]

    @pl.when(step == 0)
    def _():
        for k in range(N):
            fetch(k).wait()

    floats = x_ref[...].reshape(MERGE_ROWS, VD).astype(f32)
    mixed = floats + dot(heads_s[...], wo_s[...], (0, 0))
    merged = normed_rows(mixed, gain_ref[...]).astype(bf16)
    split = merged.reshape(MERGE_ROWS // LOCAL, 4, LOCAL // 4, VD)
    rows = pl.ds(pl.multiple_of(step * MERGE_TOK, MERGE_TOK), MERGE_TOK)
    for a in range(4):
        merged_s[rows, a * VD : (a + 1) * VD] = split[:, a].reshape(MERGE_TOK, VD)

    @pl.when(step == MERGE_STEPS - 1)
    def _():
        weights.wait()
        visual = dot(merged_s[...], wm_s[...], (1, 0)).astype(bf16).astype(f32)
        squares = row_of(jnp.sum(visual * visual, axis=1, keepdims=True))
        zeros = jnp.zeros((CHUNK - 67, VTOK), f32)
        extra = jnp.concatenate([*three_parts(squares), zeros], axis=0)
        gained = (visual * kg_ref[...]).astype(bf16)
        kv = dot(wk_ref[...], gained, (1, 1))
        for v in range(N):
            both = jnp.concatenate([kv[64 * v : 64 * v + 64, :], extra], axis=0)
            out_ref[v, :, :] = both.astype(bf16)


def merge(order, pieces, x, gain, w_merge, kv_gain, w_kv):
    whole = lambda i, order: (0, 0)
    grid_spec = pltpu.PrefetchScalarGridSpec(
        num_scalar_prefetch=1,
        grid=(MERGE_STEPS,),
        in_specs=[
            pl.BlockSpec((piece.shape[0], MERGE_ROWS), lambda i, order: (0, i)) for piece in pieces
        ]
        + [
            pl.BlockSpec((N // MERGE_STEPS, LOCAL, VD), lambda i, order: (i, 0, 0)),
            pl.BlockSpec(memory_space=pl.ANY),
            pl.BlockSpec((1, VD), whole),
            pl.BlockSpec(memory_space=pl.ANY),
            pl.BlockSpec((1, 512), whole),
            pl.BlockSpec((1024, 512), whole),
        ],
        out_specs=pl.BlockSpec((N, CHUNK, VTOK), lambda i, order: (0, 0, 0)),
        scratch_shapes=[
            pltpu.VMEM((VD, MERGE_ROWS), bf16),
            pltpu.VMEM((VTOK, 4 * VD), bf16),
            pltpu.VMEM((VD, VD), bf16),
            pltpu.VMEM((4 * VD, 512), bf16),
            pltpu.SemaphoreType.DMA((N,)),
            pltpu.SemaphoreType.DMA,
        ],
    )
    return pl.pallas_call(
        merge_kernel,
        grid_spec=grid_spec,
        out_shape=jax.ShapeDtypeStruct((N, CHUNK, VTOK), bf16),
        compiler_params=pltpu.CompilerParams(vmem_limit_bytes=56 * 2**20),
        name="merge",
    )(order, *pieces, x, x, gain, w_merge, kv_gain, w_kv)


PACK = 272
PER = 8
SCALE2 = LOG2E / math.sqrt(HD)


def response_kernel(qa_ref, qb_ref, kv_ref, ones_ref, mask_ref, out_ref):
    values = jnp.concatenate([kv_ref[HD:, :], ones_ref[...]], axis=0)
    for r in range(PER):
        qa, qb = qa_ref[r], qb_ref[r]
        query = jnp.concatenate([qa[:, :HD], qb[:, :HD], qa[:, HD:], qb[:, HD:]], axis=0)
        scores = dot(query, kv_ref[:HD, :], (1, 0)) + mask_ref[...]
        highest = jnp.max(scores, axis=1, keepdims=True)
        expo = jnp.exp2((scores - highest) * SCALE2).astype(bf16)
        mixed = dot(expo, values, (1, 1))
        total = mixed[:, HD : HD + 1]
        out_ref[r, : 2 * R_TOK, :] = (mixed[:, :HD] / total).astype(bf16)
        level = row_of(highest * SCALE2 + jnp.log2(total))
        parts = [part[:, k * HD : k * HD + HD] for part in three_parts(level) for k in range(2)]
        tail = jnp.concatenate(parts + [jnp.zeros((10, HD), f32)], axis=0)
        out_ref[r, 2 * R_TOK :, :] = tail.astype(bf16)


def response(qa, qb, kv, mask):
    whole = lambda i: (0, 0)
    some = lambda i: (i, 0, 0)
    keys = CROWS + VTOK
    return pl.pallas_call(
        response_kernel,
        grid=(N // PER,),
        in_specs=[
            pl.BlockSpec((PER, R_TOK // 2, 2 * HD), some),
            pl.BlockSpec((PER, R_TOK // 2, 2 * HD), some),
            pl.BlockSpec((2 * HD, keys), whole),
            pl.BlockSpec((HD, keys), whole),
            pl.BlockSpec((1, keys), whole),
        ],
        out_specs=pl.BlockSpec((PER, PACK, HD), some),
        out_shape=jax.ShapeDtypeStruct((N, PACK, HD), bf16),
        compiler_params=pltpu.CompilerParams(vmem_limit_bytes=48 * 2**20),
        name="response",
    )(qa, qb, kv, jnp.ones((HD, keys), bf16), mask)


def place_kernel(order_ref, *refs):
    out_ref = refs[-1]
    for k in range(N):
        first = pl.multiple_of(order_ref[k] * 2 * HD, 2 * HD)
        out_ref[:, pl.ds(first, 2 * HD)] = refs[k][...]


def placed(order, pieces):
    whole = lambda i, order: (0, 0)
    grid_spec = pltpu.PrefetchScalarGridSpec(
        num_scalar_prefetch=1,
        grid=(1,),
        in_specs=[pl.BlockSpec((R_TOK, 2 * HD), whole)] * N,
        out_specs=pl.BlockSpec((R_TOK, QH * HD), whole),
    )
    return pl.pallas_call(
        place_kernel,
        grid_spec=grid_spec,
        out_shape=jax.ShapeDtypeStruct((R_TOK, QH * HD), bf16),
        name="placed",
    )(order, *pieces)


def per_device(
    patches,
    vis_gain,
    w_qkv,
    w_out,
    merge_gain,
    w_merge,
    token_dest,
    token_row,
    prompt_text,
    kv_gain,
    w_kv,
    queries,
    resp_kv,
    resp_len,
):
    ctx_index = lax.axis_index("ctx")
    vis_index = lax.axis_index("vis")
    group = vis_index // 4

    rows = jnp.arange(LOCAL + VHD, dtype=jnp.int32)
    source = jnp.where(rows < LOCAL, rows % 32 * 4 + rows // 32, -1)
    from_patches = (source[:, None] == jnp.arange(LOCAL, dtype=jnp.int32)[None, :]).astype(bf16)
    from_out = (rows[:, None] - LOCAL == jnp.arange(VHD, dtype=jnp.int32)[None, :]).astype(bf16)
    block = dot(from_patches, patches, (1, 0)) + dot(from_out, w_out, (1, 0))
    image = lax.all_gather(block.astype(bf16), "vis", axis=0)
    w_turned = jnp.transpose(w_qkv, (1, 0))

    w_kv_mine = w_kv.T.reshape(2, KVH, 2, 64, 512).transpose(1, 0, 2, 3, 4).reshape(1024, 512)
    text = prompt_text.astype(f32)
    text_squares = jnp.sum(text * text, axis=1)
    text_gained = (text * kv_gain).astype(bf16)
    text_part = dot(w_kv_mine, text_gained, (1, 1)).reshape(N, 64, CROWS)
    text_extra = jnp.broadcast_to(text_squares[None, None, :], (N, 8, CROWS))
    text_part = jnp.concatenate([text_part, text_extra], axis=1).reshape(N * CHUNK, CROWS)

    own_q = lax.dynamic_slice_in_dim(queries, vis_index * 256, 256, 1)
    vis_row = vis_gain.reshape(1, VD)
    merge_row = merge_gain.reshape(1, VD)
    owners = ring_owners(vis_index)
    own_q, text_part, vis_row, merge_row, owners = lax.optimization_barrier(
        (own_q, text_part, vis_row, merge_row, owners)
    )
    half = R_TOK // 2
    qa = lax.all_gather(own_q[:half], "ctx", axis=0)
    qb = lax.all_gather(own_q[half:], "ctx", axis=0)

    flat_dest = token_dest.reshape(-1)
    flat_row = token_row.reshape(-1)
    here = jnp.where(flat_dest == ctx_index, flat_row // 128, -1)
    tall = (here[None, :] == jnp.arange(8, dtype=jnp.int32)[:, None]).astype(bf16)
    wide = ((flat_row % 128)[:, None] == jnp.arange(128, dtype=jnp.int32)[None, :]).astype(bf16)
    taken = dot(tall, wide, (1, 0)).reshape(1, CROWS)
    mask = jnp.where(taken > 0.5, NEG, 0.0)
    mask = jnp.concatenate([mask, jnp.zeros((1, VTOK), f32)], axis=1)

    own_k = lax.dynamic_slice_in_dim(resp_kv, group * HD, HD, 1)
    own_v = lax.dynamic_slice_in_dim(resp_kv, KVH * HD + group * HD, HD, 1)
    positions = jnp.arange(R_TOK, dtype=jnp.int32)
    visible = positions[None, :] <= positions[:, None]
    q_two = own_q.reshape(R_TOK, 2, HD)
    own_scores = jnp.einsum("rhd,nd->hrn", q_two, own_k, preferred_element_type=f32)
    own_scores = jnp.where(visible, own_scores * (1.0 / math.sqrt(HD)), NEG)
    own_high = jnp.max(own_scores, axis=2, keepdims=True)
    own_expo = jnp.where(visible, jnp.exp(own_scores - own_high), 0.0)
    own_total = jnp.sum(own_expo, axis=2, keepdims=True)
    own_mixed = jnp.einsum("hrn,nd->hrd", own_expo.astype(bf16), own_v, preferred_element_type=f32)
    own_mixed = (own_mixed / own_total).reshape(256, HD)
    own_level = (own_high * LOG2E + jnp.log2(own_total)).reshape(1, 256)

    image, qa, qb, text_part = lax.optimization_barrier((image, qa, qb, text_part))
    own_heads = vision(image, vis_row, w_turned)
    text_sum = lax.psum_scatter(text_part, "vis", scatter_dimension=0, tiled=True)
    text_scale = lax.rsqrt(text_sum[64:65] / D + EPS)
    text_kv = (text_sum[:64] * text_scale).astype(bf16)
    partial = merge(
        owners,
        ring_gather(own_heads),
        image,
        merge_row,
        w_merge,
        kv_gain.reshape(1, 512),
        w_kv_mine,
    )
    arrived = lax.all_to_all(partial, "vis", split_axis=0, concat_axis=0, tiled=True)
    arrived, text_kv = lax.optimization_barrier((arrived, text_kv))
    vis_sum = jnp.sum(arrived.astype(f32), axis=0)
    vis_squares = vis_sum[64:65] + vis_sum[65:66] + vis_sum[66:67]
    vis_kv = (vis_sum[:64] * lax.rsqrt(vis_squares / D + EPS)).astype(bf16)
    kv = jnp.concatenate([text_kv, vis_kv], axis=1)
    kv = lax.all_gather(kv, "vis", axis=0, tiled=True, axis_index_groups=QUADS)
    packed = response(qa, qb, kv, mask)
    back = lax.all_to_all(packed, "ctx", split_axis=0, concat_axis=0, tiled=True).astype(f32)
    levels = back[:, 256:258] + back[:, 258:260] + back[:, 260:262]
    levels = levels.reshape(N, 256)
    highest = jnp.maximum(jnp.max(levels, axis=0, keepdims=True), own_level)
    weights = jnp.exp2(levels - highest)
    own_weight = jnp.exp2(own_level - highest)
    total = jnp.sum(weights, axis=0, keepdims=True) + own_weight
    weights = weights / total
    own_weight = own_weight / total
    result = jnp.sum(back[:, :256] * weights[:, :, None], axis=0)
    result = result + own_mixed * own_weight.reshape(256, 1)
    result = jnp.transpose(result.reshape(2, R_TOK, HD), (1, 0, 2)).reshape(R_TOK, 256)
    live = (positions < resp_len[0])[:, None]
    result = jnp.where(live, result, 0.0).astype(bf16)
    return placed(owners, short_gather(result))


def solution(mesh):
    return jax.shard_map(
        per_device,
        mesh=mesh,
        in_specs=(
            P(("ctx", "vis"), None),
            P(),
            P(None, "vis"),
            P("vis", None),
            P(),
            P(None, "vis"),
            P(),
            P(),
            P("ctx", "vis"),
            P("vis"),
            P("vis", None),
            P("ctx", None),
            P("ctx", None),
            P("ctx"),
        ),
        out_specs=P("ctx", None),
        check_vma=False,
    )
```

```python
import math

import jax
import jax.numpy as jnp
from jax import lax
from jax.experimental import pallas as pl
from jax.experimental.pallas import tpu as pltpu
from jax.sharding import PartitionSpec as P

VD = 1280
VHEADS = 16
D = 8192
HD = 128
QH = 32
KVH = 4
CROWS = 1024
R_TOK = 128
VHD = 80
GP = 2048
VTOK = 512
N = 16
LOCAL = GP // N
EPS = 1e-06
NEG = -1e30
bf16 = jnp.bfloat16
f32 = jnp.float32

QUADS = [[4 * g + i for i in range(4)] for g in range(4)]
LOG2E = math.log2(math.e)


def onward(block, hops=1):
    pairs = [(2 * z, 2 * ((z + hops) % 8)) for z in range(8)]
    pairs += [(2 * z + 1, 2 * ((z - hops) % 8) + 1) for z in range(8)]
    return lax.ppermute(block, "vis", pairs)


def swapped(block):
    return lax.ppermute(block, "vis", [(i, i ^ 1) for i in range(N)])


def ring_gather(block):
    same = [block]
    other = [swapped(block)]
    for step in range(3):
        same.append(onward(same[-1]))
        other.append(onward(other[-1]))
    same.append(onward(same[-1]))
    away = [swapped(piece) for piece in same[1:]]
    back = [swapped(piece) for piece in other[1:]]
    return same + other + away + back


def short_gather(block):
    same = [block, onward(block), onward(block, 2)]
    first = swapped(block)
    other = [first, onward(first), onward(first, 2)]
    same += [onward(same[1], 2), onward(same[2], 2)]
    other += [onward(other[1], 2)]
    away = [swapped(piece) for piece in same[1:]]
    back = [swapped(piece) for piece in other[1:]]
    return same + other + away + back


def ring_owners(vis_index):
    z = vis_index // 2
    core = vis_index % 2
    sign = 2 * core - 1
    hops = jnp.array((0, 1, 2, 3, 4, 0, 1, 2, 3, -1, -2, -3, -4, -1, -2, -3), jnp.int32)
    flips = jnp.array((0,) * 5 + (1,) * 4 + (1,) * 4 + (0,) * 3, jnp.int32)
    return (z + sign * hops) % 8 * 2 + (core + flips) % 2


def dot(a, b, contract):
    return lax.dot_general(a, b, ((contract[:1], contract[1:]), ((), ())), preferred_element_type=f32)


def normed_rows(values, gain):
    center = values - jnp.mean(values, axis=-1, keepdims=True)
    spread = jnp.mean(center * center, axis=-1, keepdims=True)
    return center * lax.rsqrt(spread + EPS) * gain


QKV_STEPS = 4
QKV_ROWS = GP // QKV_STEPS
QKV_PART = 256
ATT_STEPS = 2
ATT_ROWS = GP // ATT_STEPS
ATT_PART = 256


def vision_kernel(x_ref, gain_ref, w_ref, out_ref, w_s, q_s, k_s, v_s):
    step = pl.program_id(0)

    @pl.when(step == 0)
    def _():
        for part in range(3):
            w_s[part * 128 : part * 128 + VHD, :] = w_ref[part * VHD : part * VHD + VHD, :]
            w_s[part * 128 + VHD : part * 128 + 128, :] = jnp.zeros((128 - VHD, VD), bf16)

    @pl.when(step < QKV_STEPS)
    def _():
        count = QKV_PART // LOCAL
        for part in range(0, QKV_ROWS // LOCAL, count):
            rows = x_ref[part : part + count].reshape(QKV_PART, VD)
            normed = normed_rows(rows.astype(f32), gain_ref[...]).astype(bf16)
            qkv = dot(normed, w_s[...], (1, 1)).astype(bf16)
            first = step * QKV_ROWS + part * LOCAL
            rows = pl.ds(pl.multiple_of(first, QKV_PART), QKV_PART)
            q_s[rows, :] = qkv[:, :128]
            k_s[rows, :] = qkv[:, 128:256]
            lane = lax.broadcasted_iota(jnp.int32, (QKV_PART, 128), 1)
            v_s[rows, :] = jnp.where(lane == VHD, jnp.ones((), bf16), qkv[:, 256:])

    @pl.when(step >= QKV_STEPS)
    def _():
        first = pl.multiple_of((step - QKV_STEPS) * ATT_ROWS, ATT_ROWS)
        for part in range(0, ATT_ROWS, ATT_PART):
            query = q_s[pl.ds(first + part, ATT_PART), :]
            scores = dot(query, k_s[...], (1, 1))
            highest = jnp.max(scores, axis=1, keepdims=True)
            expo = jnp.exp2((scores - highest) * (LOG2E / math.sqrt(VHD))).astype(bf16)
            mixed = dot(expo, v_s[...], (1, 0))
            mixed = mixed / mixed[:, VHD : VHD + 1]
            out_ref[:, part : part + ATT_PART] = jnp.transpose(mixed, (1, 0))[:VHD, :].astype(bf16)


def vision(x, gain, w):
    return pl.pallas_call(
        vision_kernel,
        grid=(QKV_STEPS + ATT_STEPS,),
        in_specs=[
            pl.BlockSpec((N // QKV_STEPS, LOCAL, VD), lambda i: (jnp.minimum(i, QKV_STEPS - 1), 0, 0)),
            pl.BlockSpec((1, VD), lambda i: (0, 0)),
            pl.BlockSpec((3 * VHD, VD), lambda i: (0, 0)),
        ],
        out_specs=pl.BlockSpec((VHD, ATT_ROWS), lambda i: (0, jnp.maximum(i - QKV_STEPS, 0))),
        out_shape=jax.ShapeDtypeStruct((VHD, GP), bf16),
        scratch_shapes=[pltpu.VMEM((384, VD), bf16)] + [pltpu.VMEM((GP, 128), bf16)] * 3,
        compiler_params=pltpu.CompilerParams(vmem_limit_bytes=60 * 2**20),
        name="vision",
    )(x, gain, w)


MERGE_STEPS = 4
MERGE_ROWS = GP // MERGE_STEPS
MERGE_TOK = VTOK // MERGE_STEPS
MERGE_PART = 256
CHUNK = 72
HELD = N


def row_of(column):
    count = column.shape[0]
    down = lax.broadcasted_iota(jnp.int32, (count, count), 0)
    across = lax.broadcasted_iota(jnp.int32, (count, count), 1)
    return jnp.sum(jnp.where(down == across, column, 0.0), axis=0, keepdims=True)


def three_parts(row):
    high = row.astype(bf16).astype(f32)
    middle = (row - high).astype(bf16).astype(f32)
    return high, middle, row - high - middle


def merge_kernel(order_ref, *refs):
    pieces = refs[:HELD]
    x_ref, all_ref, gain_ref, wm_ref, kg_ref, wk_ref, out_ref = refs[HELD : HELD + 7]
    heads_s, merged_s, wo_s, wm_s, sems, wm_sem = refs[HELD + 7 :]
    step = pl.program_id(0)

    def fetch(k):
        source = all_ref.at[k, pl.ds(LOCAL, VHD), :]
        return pltpu.make_async_copy(source, wo_s.at[pl.ds(k * VHD, VHD), :], sems.at[k])

    weights = pltpu.make_async_copy(wm_ref, wm_s, wm_sem)

    @pl.when(step == 0)
    def _():
        for k in range(N):
            fetch(k).start()
        weights.start()

    for k in range(N):
        first = pl.multiple_of(order_ref[k] * VHD, VHD)
        heads_s[pl.ds(first, VHD), :] = pieces[k][...]

    @pl.when(step == 0)
    def _():
        for k in range(N):
            fetch(k).wait()

    count = MERGE_PART // LOCAL
    for part in range(0, MERGE_ROWS // LOCAL, count):
        floats = x_ref[part : part + count].reshape(MERGE_PART, VD).astype(f32)
        heads = heads_s[:, part * LOCAL : (part + count) * LOCAL]
        mixed = floats + dot(heads, wo_s[...], (0, 0))
        merged = normed_rows(mixed, gain_ref[...]).astype(bf16)
        split = merged.reshape(count, 4, LOCAL // 4, VD)
        first = step * MERGE_TOK + part * LOCAL // 4
        rows = pl.ds(pl.multiple_of(first, MERGE_PART // 4), MERGE_PART // 4)
        for a in range(4):
            merged_s[rows, a * VD : (a + 1) * VD] = split[:, a].reshape(MERGE_PART // 4, VD)

    @pl.when(step == MERGE_STEPS - 1)
    def _():
        weights.wait()
        visual = dot(merged_s[...], wm_s[...], (1, 0)).astype(bf16).astype(f32)
        squares = row_of(jnp.sum(visual * visual, axis=1, keepdims=True))
        zeros = jnp.zeros((CHUNK - 67, VTOK), f32)
        extra = jnp.concatenate([*three_parts(squares), zeros], axis=0)
        gained = (visual * kg_ref[...]).astype(bf16)
        kv = dot(wk_ref[...], gained, (1, 1))
        for v in range(N):
            both = jnp.concatenate([kv[64 * v : 64 * v + 64, :], extra], axis=0)
            out_ref[v, :, :] = both.astype(bf16)


def merge(order, pieces, x, gain, w_merge, kv_gain, w_kv):
    whole = lambda i, order: (0, 0)
    grid_spec = pltpu.PrefetchScalarGridSpec(
        num_scalar_prefetch=1,
        grid=(MERGE_STEPS,),
        in_specs=[
            pl.BlockSpec((piece.shape[0], MERGE_ROWS), lambda i, order: (0, i)) for piece in pieces
        ]
        + [
            pl.BlockSpec((N // MERGE_STEPS, LOCAL, VD), lambda i, order: (i, 0, 0)),
            pl.BlockSpec(memory_space=pl.ANY),
            pl.BlockSpec((1, VD), whole),
            pl.BlockSpec(memory_space=pl.ANY),
            pl.BlockSpec((1, 512), whole),
            pl.BlockSpec((1024, 512), whole),
        ],
        out_specs=pl.BlockSpec((N, CHUNK, VTOK), lambda i, order: (0, 0, 0)),
        scratch_shapes=[
            pltpu.VMEM((VD, MERGE_ROWS), bf16),
            pltpu.VMEM((VTOK, 4 * VD), bf16),
            pltpu.VMEM((VD, VD), bf16),
            pltpu.VMEM((4 * VD, 512), bf16),
            pltpu.SemaphoreType.DMA((N,)),
            pltpu.SemaphoreType.DMA,
        ],
    )
    return pl.pallas_call(
        merge_kernel,
        grid_spec=grid_spec,
        out_shape=jax.ShapeDtypeStruct((N, CHUNK, VTOK), bf16),
        compiler_params=pltpu.CompilerParams(vmem_limit_bytes=56 * 2**20),
        name="merge",
    )(order, *pieces, x, x, gain, w_merge, kv_gain, w_kv)


PACK = 272
PER = 8
SCALE2 = LOG2E / math.sqrt(HD)


def response_kernel(qa_ref, qb_ref, kv_ref, ones_ref, mask_ref, out_ref):
    values = jnp.concatenate([kv_ref[HD:, :], ones_ref[...]], axis=0)
    for r in range(PER):
        qa, qb = qa_ref[r], qb_ref[r]
        query = jnp.concatenate([qa[:, :HD], qb[:, :HD], qa[:, HD:], qb[:, HD:]], axis=0)
        scores = dot(query, kv_ref[:HD, :], (1, 0)) + mask_ref[...]
        highest = jnp.max(scores, axis=1, keepdims=True)
        expo = jnp.exp2((scores - highest) * SCALE2).astype(bf16)
        mixed = dot(expo, values, (1, 1))
        total = mixed[:, HD : HD + 1]
        out_ref[r, : 2 * R_TOK, :] = (mixed[:, :HD] / total).astype(bf16)
        level = row_of(highest * SCALE2 + jnp.log2(total))
        parts = [part[:, k * HD : k * HD + HD] for part in three_parts(level) for k in range(2)]
        tail = jnp.concatenate(parts + [jnp.zeros((10, HD), f32)], axis=0)
        out_ref[r, 2 * R_TOK :, :] = tail.astype(bf16)


def response(qa, qb, kv, mask):
    whole = lambda i: (0, 0)
    some = lambda i: (i, 0, 0)
    keys = CROWS + VTOK
    return pl.pallas_call(
        response_kernel,
        grid=(N // PER,),
        in_specs=[
            pl.BlockSpec((PER, R_TOK // 2, 2 * HD), some),
            pl.BlockSpec((PER, R_TOK // 2, 2 * HD), some),
            pl.BlockSpec((2 * HD, keys), whole),
            pl.BlockSpec((HD, keys), whole),
            pl.BlockSpec((1, keys), whole),
        ],
        out_specs=pl.BlockSpec((PER, PACK, HD), some),
        out_shape=jax.ShapeDtypeStruct((N, PACK, HD), bf16),
        compiler_params=pltpu.CompilerParams(vmem_limit_bytes=48 * 2**20),
        name="response",
    )(qa, qb, kv, jnp.ones((HD, keys), bf16), mask)


def place_kernel(order_ref, *refs):
    out_ref = refs[-1]
    for k in range(N):
        first = pl.multiple_of(order_ref[k] * 2 * HD, 2 * HD)
        out_ref[:, pl.ds(first, 2 * HD)] = refs[k][...]


def placed(order, pieces):
    whole = lambda i, order: (0, 0)
    grid_spec = pltpu.PrefetchScalarGridSpec(
        num_scalar_prefetch=1,
        grid=(1,),
        in_specs=[pl.BlockSpec((R_TOK, 2 * HD), whole)] * N,
        out_specs=pl.BlockSpec((R_TOK, QH * HD), whole),
    )
    return pl.pallas_call(
        place_kernel,
        grid_spec=grid_spec,
        out_shape=jax.ShapeDtypeStruct((R_TOK, QH * HD), bf16),
        name="placed",
    )(order, *pieces)


def per_device(
    patches,
    vis_gain,
    w_qkv,
    w_out,
    merge_gain,
    w_merge,
    token_dest,
    token_row,
    prompt_text,
    kv_gain,
    w_kv,
    queries,
    resp_kv,
    resp_len,
):
    ctx_index = lax.axis_index("ctx")
    vis_index = lax.axis_index("vis")
    group = vis_index // 4

    rows = jnp.arange(LOCAL + VHD, dtype=jnp.int32)
    source = jnp.where(rows < LOCAL, rows % 32 * 4 + rows // 32, -1)
    from_patches = (source[:, None] == jnp.arange(LOCAL, dtype=jnp.int32)[None, :]).astype(bf16)
    from_out = (rows[:, None] - LOCAL == jnp.arange(VHD, dtype=jnp.int32)[None, :]).astype(bf16)
    block = dot(from_patches, patches, (1, 0)) + dot(from_out, w_out, (1, 0))
    image = lax.all_gather(block.astype(bf16), "vis", axis=0)
    w_turned = jnp.transpose(w_qkv, (1, 0))

    w_kv_mine = w_kv.T.reshape(2, KVH, 2, 64, 512).transpose(1, 0, 2, 3, 4).reshape(1024, 512)
    text = prompt_text.astype(f32)
    text_squares = jnp.sum(text * text, axis=1)
    text_gained = (text * kv_gain).astype(bf16)
    text_part = dot(w_kv_mine, text_gained, (1, 1)).reshape(N, 64, CROWS)
    text_extra = jnp.broadcast_to(text_squares[None, None, :], (N, 8, CROWS))
    text_part = jnp.concatenate([text_part, text_extra], axis=1).reshape(N * CHUNK, CROWS)

    own_q = lax.dynamic_slice_in_dim(queries, vis_index * 256, 256, 1)
    vis_row = vis_gain.reshape(1, VD)
    merge_row = merge_gain.reshape(1, VD)
    owners = ring_owners(vis_index)
    own_q, text_part, vis_row, merge_row, owners = lax.optimization_barrier(
        (own_q, text_part, vis_row, merge_row, owners)
    )
    half = R_TOK // 2
    qa = lax.all_gather(own_q[:half], "ctx", axis=0)
    qb = lax.all_gather(own_q[half:], "ctx", axis=0)

    flat_dest = token_dest.reshape(-1)
    flat_row = token_row.reshape(-1)
    here = jnp.where(flat_dest == ctx_index, flat_row // 128, -1)
    tall = (here[None, :] == jnp.arange(8, dtype=jnp.int32)[:, None]).astype(bf16)
    wide = ((flat_row % 128)[:, None] == jnp.arange(128, dtype=jnp.int32)[None, :]).astype(bf16)
    taken = dot(tall, wide, (1, 0)).reshape(1, CROWS)
    mask = jnp.where(taken > 0.5, NEG, 0.0)
    mask = jnp.concatenate([mask, jnp.zeros((1, VTOK), f32)], axis=1)

    own_k = lax.dynamic_slice_in_dim(resp_kv, group * HD, HD, 1)
    own_v = lax.dynamic_slice_in_dim(resp_kv, KVH * HD + group * HD, HD, 1)
    positions = jnp.arange(R_TOK, dtype=jnp.int32)
    visible = positions[None, :] <= positions[:, None]
    q_two = own_q.reshape(R_TOK, 2, HD)
    own_scores = jnp.einsum("rhd,nd->hrn", q_two, own_k, preferred_element_type=f32)
    own_scores = jnp.where(visible, own_scores * (1.0 / math.sqrt(HD)), NEG)
    own_high = jnp.max(own_scores, axis=2, keepdims=True)
    own_expo = jnp.where(visible, jnp.exp(own_scores - own_high), 0.0)
    own_total = jnp.sum(own_expo, axis=2, keepdims=True)
    own_mixed = jnp.einsum("hrn,nd->hrd", own_expo.astype(bf16), own_v, preferred_element_type=f32)
    own_mixed = (own_mixed / own_total).reshape(256, HD)
    own_level = (own_high * LOG2E + jnp.log2(own_total)).reshape(1, 256)

    image, qa, qb, text_part = lax.optimization_barrier((image, qa, qb, text_part))
    own_heads = vision(image, vis_row, w_turned)
    text_sum = lax.psum_scatter(text_part, "vis", scatter_dimension=0, tiled=True)
    text_scale = lax.rsqrt(text_sum[64:65] / D + EPS)
    text_kv = (text_sum[:64] * text_scale).astype(bf16)
    partial = merge(
        owners,
        ring_gather(own_heads),
        image,
        merge_row,
        w_merge,
        kv_gain.reshape(1, 512),
        w_kv_mine,
    )
    arrived = lax.all_to_all(partial, "vis", split_axis=0, concat_axis=0, tiled=True)
    arrived, text_kv = lax.optimization_barrier((arrived, text_kv))
    vis_sum = jnp.sum(arrived.astype(f32), axis=0)
    vis_squares = vis_sum[64:65] + vis_sum[65:66] + vis_sum[66:67]
    vis_kv = (vis_sum[:64] * lax.rsqrt(vis_squares / D + EPS)).astype(bf16)
    kv = jnp.concatenate([text_kv, vis_kv], axis=1)
    kv = lax.all_gather(kv, "vis", axis=0, tiled=True, axis_index_groups=QUADS)
    packed = response(qa, qb, kv, mask)
    back = lax.all_to_all(packed, "ctx", split_axis=0, concat_axis=0, tiled=True).astype(f32)
    levels = back[:, 256:258] + back[:, 258:260] + back[:, 260:262]
    levels = levels.reshape(N, 256)
    highest = jnp.maximum(jnp.max(levels, axis=0, keepdims=True), own_level)
    weights = jnp.exp2(levels - highest)
    own_weight = jnp.exp2(own_level - highest)
    total = jnp.sum(weights, axis=0, keepdims=True) + own_weight
    weights = weights / total
    own_weight = own_weight / total
    result = jnp.sum(back[:, :256] * weights[:, :, None], axis=0)
    result = result + own_mixed * own_weight.reshape(256, 1)
    result = jnp.transpose(result.reshape(2, R_TOK, HD), (1, 0, 2)).reshape(R_TOK, 256)
    live = (positions < resp_len[0])[:, None]
    result = jnp.where(live, result, 0.0).astype(bf16)
    return placed(owners, short_gather(result))


def solution(mesh):
    return jax.shard_map(
        per_device,
        mesh=mesh,
        in_specs=(
            P(("ctx", "vis"), None),
            P(),
            P(None, "vis"),
            P("vis", None),
            P(),
            P(None, "vis"),
            P(),
            P(),
            P("ctx", "vis"),
            P("vis"),
            P("vis", None),
            P("ctx", None),
            P("ctx", None),
            P("ctx"),
        ),
        out_specs=P("ctx", None),
        check_vma=False,
    )
```

```python
import math

import jax
import jax.numpy as jnp
from jax import lax
from jax.experimental import pallas as pl
from jax.experimental.pallas import tpu as pltpu
from jax.sharding import PartitionSpec as P

VD = 1280
VHEADS = 16
D = 8192
HD = 128
QH = 32
KVH = 4
CROWS = 1024
R_TOK = 128
VHD = 80
GP = 2048
VTOK = 512
N = 16
LOCAL = GP // N
EPS = 1e-06
NEG = -1e30
bf16 = jnp.bfloat16
f32 = jnp.float32

QUADS = [[4 * g + i for i in range(4)] for g in range(4)]
LOG2E = math.log2(math.e)


def onward(block, hops=1):
    pairs = [(2 * z, 2 * ((z + hops) % 8)) for z in range(8)]
    pairs += [(2 * z + 1, 2 * ((z - hops) % 8) + 1) for z in range(8)]
    return lax.ppermute(block, "vis", pairs)


def swapped(block):
    return lax.ppermute(block, "vis", [(i, i ^ 1) for i in range(N)])


def ring_gather(block):
    same = [block]
    other = [swapped(block)]
    for step in range(3):
        same.append(onward(same[-1]))
        other.append(onward(other[-1]))
    same.append(onward(same[-1]))
    away = [swapped(piece) for piece in same[1:]]
    back = [swapped(piece) for piece in other[1:]]
    return same + other + away + back


def short_gather(block):
    same = [block, onward(block), onward(block, 2)]
    first = swapped(block)
    other = [first, onward(first), onward(first, 2)]
    same += [onward(same[1], 2), onward(same[2], 2)]
    other += [onward(other[1], 2)]
    away = [swapped(piece) for piece in same[1:]]
    back = [swapped(piece) for piece in other[1:]]
    return same + other + away + back


def ring_owners(vis_index):
    z = vis_index // 2
    core = vis_index % 2
    sign = 2 * core - 1
    hops = jnp.array((0, 1, 2, 3, 4, 0, 1, 2, 3, -1, -2, -3, -4, -1, -2, -3), jnp.int32)
    flips = jnp.array((0,) * 5 + (1,) * 4 + (1,) * 4 + (0,) * 3, jnp.int32)
    return (z + sign * hops) % 8 * 2 + (core + flips) % 2


def dot(a, b, contract):
    return lax.dot_general(a, b, ((contract[:1], contract[1:]), ((), ())), preferred_element_type=f32)


def normed_rows(values, gain):
    center = values - jnp.mean(values, axis=-1, keepdims=True)
    spread = jnp.mean(center * center, axis=-1, keepdims=True)
    return center * lax.rsqrt(spread + EPS) * gain


QKV_STEPS = 4
QKV_ROWS = GP // QKV_STEPS
QKV_PART = 256
ATT_STEPS = 2
ATT_ROWS = GP // ATT_STEPS
ATT_PART = 256


def vision_kernel(x_ref, gain_ref, w_ref, out_ref, w_s, q_s, k_s, v_s):
    step = pl.program_id(0)

    @pl.when(step == 0)
    def _():
        for part in range(3):
            w_s[part * 128 : part * 128 + VHD, :] = w_ref[part * VHD : part * VHD + VHD, :]
            w_s[part * 128 + VHD : part * 128 + 128, :] = jnp.zeros((128 - VHD, VD), bf16)

    @pl.when(step < QKV_STEPS)
    def _():
        count = QKV_PART // LOCAL
        for part in range(0, QKV_ROWS // LOCAL, count):
            rows = x_ref[part : part + count].reshape(QKV_PART, VD)
            normed = normed_rows(rows.astype(f32), gain_ref[...]).astype(bf16)
            qkv = dot(normed, w_s[...], (1, 1)).astype(bf16)
            first = step * QKV_ROWS + part * LOCAL
            rows = pl.ds(pl.multiple_of(first, QKV_PART), QKV_PART)
            q_s[rows, :] = qkv[:, :128]
            k_s[rows, :] = qkv[:, 128:256]
            lane = lax.broadcasted_iota(jnp.int32, (QKV_PART, 128), 1)
            v_s[rows, :] = jnp.where(lane == VHD, jnp.ones((), bf16), qkv[:, 256:])

    @pl.when(step >= QKV_STEPS)
    def _():
        first = pl.multiple_of((step - QKV_STEPS) * ATT_ROWS, ATT_ROWS)
        for part in range(0, ATT_ROWS, ATT_PART):
            query = q_s[pl.ds(first + part, ATT_PART), :]
            scores = dot(query, k_s[...], (1, 1))
            highest = jnp.max(scores, axis=1, keepdims=True)
            expo = jnp.exp2((scores - highest) * (LOG2E / math.sqrt(VHD))).astype(bf16)
            mixed = dot(expo, v_s[...], (1, 0))
            mixed = mixed / mixed[:, VHD : VHD + 1]
            out_ref[:, part : part + ATT_PART] = jnp.transpose(mixed, (1, 0))[:VHD, :].astype(bf16)


def vision(x, gain, w):
    return pl.pallas_call(
        vision_kernel,
        grid=(QKV_STEPS + ATT_STEPS,),
        in_specs=[
            pl.BlockSpec((N // QKV_STEPS, LOCAL, VD), lambda i: (jnp.minimum(i, QKV_STEPS - 1), 0, 0)),
            pl.BlockSpec((1, VD), lambda i: (0, 0)),
            pl.BlockSpec((3 * VHD, VD), lambda i: (0, 0)),
        ],
        out_specs=pl.BlockSpec((VHD, ATT_ROWS), lambda i: (0, jnp.maximum(i - QKV_STEPS, 0))),
        out_shape=jax.ShapeDtypeStruct((VHD, GP), bf16),
        scratch_shapes=[pltpu.VMEM((384, VD), bf16)] + [pltpu.VMEM((GP, 128), bf16)] * 3,
        compiler_params=pltpu.CompilerParams(vmem_limit_bytes=60 * 2**20),
        name="vision",
    )(x, gain, w)


MERGE_STEPS = 4
MERGE_ROWS = GP // MERGE_STEPS
MERGE_TOK = VTOK // MERGE_STEPS
MERGE_PART = 256
CHUNK = 72
HELD = N


def row_of(column):
    count = column.shape[0]
    down = lax.broadcasted_iota(jnp.int32, (count, count), 0)
    across = lax.broadcasted_iota(jnp.int32, (count, count), 1)
    return jnp.sum(jnp.where(down == across, column, 0.0), axis=0, keepdims=True)


def three_parts(row):
    high = row.astype(bf16).astype(f32)
    middle = (row - high).astype(bf16).astype(f32)
    return high, middle, row - high - middle


def merge_kernel(order_ref, *refs):
    pieces = refs[:HELD]
    x_ref, all_ref, gain_ref, wm_ref, kg_ref, wk_ref, out_ref = refs[HELD : HELD + 7]
    heads_s, merged_s, wo_s, wm_s, sems, wm_sem = refs[HELD + 7 :]
    step = pl.program_id(0)

    def fetch(k):
        source = all_ref.at[k, pl.ds(LOCAL, VHD), :]
        return pltpu.make_async_copy(source, wo_s.at[pl.ds(k * VHD, VHD), :], sems.at[k])

    weights = pltpu.make_async_copy(wm_ref, wm_s, wm_sem)

    @pl.when(step == 0)
    def _():
        for k in range(N):
            fetch(k).start()
        weights.start()

    for k in range(N):
        first = pl.multiple_of(order_ref[k] * VHD, VHD)
        heads_s[pl.ds(first, VHD), :] = pieces[k][...]

    @pl.when(step == 0)
    def _():
        for k in range(N):
            fetch(k).wait()

    count = MERGE_PART // LOCAL
    for part in range(0, MERGE_ROWS // LOCAL, count):
        floats = x_ref[part : part + count].reshape(MERGE_PART, VD).astype(f32)
        heads = heads_s[:, part * LOCAL : (part + count) * LOCAL]
        mixed = floats + dot(heads, wo_s[...], (0, 0))
        merged = normed_rows(mixed, gain_ref[...]).astype(bf16)
        split = merged.reshape(count, 4, LOCAL // 4, VD)
        first = step * MERGE_TOK + part * LOCAL // 4
        rows = pl.ds(pl.multiple_of(first, MERGE_PART // 4), MERGE_PART // 4)
        for a in range(4):
            merged_s[rows, a * VD : (a + 1) * VD] = split[:, a].reshape(MERGE_PART // 4, VD)

    @pl.when(step == MERGE_STEPS - 1)
    def _():
        weights.wait()
        visual = dot(merged_s[...], wm_s[...], (1, 0)).astype(bf16).astype(f32)
        squares = row_of(jnp.sum(visual * visual, axis=1, keepdims=True))
        zeros = jnp.zeros((CHUNK - 67, VTOK), f32)
        extra = jnp.concatenate([*three_parts(squares), zeros], axis=0)
        gained = (visual * kg_ref[...]).astype(bf16)
        kv = dot(wk_ref[...], gained, (1, 1))
        for v in range(N):
            both = jnp.concatenate([kv[64 * v : 64 * v + 64, :], extra], axis=0)
            out_ref[v, :, :] = both.astype(bf16)


def merge(order, pieces, x, gain, w_merge, kv_gain, w_kv):
    whole = lambda i, order: (0, 0)
    grid_spec = pltpu.PrefetchScalarGridSpec(
        num_scalar_prefetch=1,
        grid=(MERGE_STEPS,),
        in_specs=[
            pl.BlockSpec((piece.shape[0], MERGE_ROWS), lambda i, order: (0, i)) for piece in pieces
        ]
        + [
            pl.BlockSpec((N // MERGE_STEPS, LOCAL, VD), lambda i, order: (i, 0, 0)),
            pl.BlockSpec(memory_space=pl.ANY),
            pl.BlockSpec((1, VD), whole),
            pl.BlockSpec(memory_space=pl.ANY),
            pl.BlockSpec((1, 512), whole),
            pl.BlockSpec((1024, 512), whole),
        ],
        out_specs=pl.BlockSpec((N, CHUNK, VTOK), lambda i, order: (0, 0, 0)),
        scratch_shapes=[
            pltpu.VMEM((VD, MERGE_ROWS), bf16),
            pltpu.VMEM((VTOK, 4 * VD), bf16),
            pltpu.VMEM((VD, VD), bf16),
            pltpu.VMEM((4 * VD, 512), bf16),
            pltpu.SemaphoreType.DMA((N,)),
            pltpu.SemaphoreType.DMA,
        ],
    )
    return pl.pallas_call(
        merge_kernel,
        grid_spec=grid_spec,
        out_shape=jax.ShapeDtypeStruct((N, CHUNK, VTOK), bf16),
        compiler_params=pltpu.CompilerParams(vmem_limit_bytes=56 * 2**20),
        name="merge",
    )(order, *pieces, x, x, gain, w_merge, kv_gain, w_kv)


PACK = 272
PER = 8
SCALE2 = LOG2E / math.sqrt(HD)


def response_kernel(qa_ref, qb_ref, kv_ref, ones_ref, mask_ref, out_ref):
    values = jnp.concatenate([kv_ref[HD:, :], ones_ref[...]], axis=0)
    for r in range(PER):
        qa, qb = qa_ref[r], qb_ref[r]
        query = jnp.concatenate([qa[:, :HD], qb[:, :HD], qa[:, HD:], qb[:, HD:]], axis=0)
        scores = dot(query, kv_ref[:HD, :], (1, 0)) + mask_ref[...]
        highest = jnp.max(scores, axis=1, keepdims=True)
        expo = jnp.exp2((scores - highest) * SCALE2).astype(bf16)
        mixed = dot(expo, values, (1, 1))
        total = mixed[:, HD : HD + 1]
        out_ref[r, : 2 * R_TOK, :] = (mixed[:, :HD] / total).astype(bf16)
        level = row_of(highest * SCALE2 + jnp.log2(total))
        parts = [part[:, k * HD : k * HD + HD] for part in three_parts(level) for k in range(2)]
        tail = jnp.concatenate(parts + [jnp.zeros((10, HD), f32)], axis=0)
        out_ref[r, 2 * R_TOK :, :] = tail.astype(bf16)


def response(qa, qb, kv, mask):
    whole = lambda i: (0, 0)
    some = lambda i: (i, 0, 0)
    keys = CROWS + VTOK
    return pl.pallas_call(
        response_kernel,
        grid=(N // PER,),
        in_specs=[
            pl.BlockSpec((PER, R_TOK // 2, 2 * HD), some),
            pl.BlockSpec((PER, R_TOK // 2, 2 * HD), some),
            pl.BlockSpec((2 * HD, keys), whole),
            pl.BlockSpec((HD, keys), whole),
            pl.BlockSpec((1, keys), whole),
        ],
        out_specs=pl.BlockSpec((PER, PACK, HD), some),
        out_shape=jax.ShapeDtypeStruct((N, PACK, HD), bf16),
        compiler_params=pltpu.CompilerParams(vmem_limit_bytes=48 * 2**20),
        name="response",
    )(qa, qb, kv, jnp.ones((HD, keys), bf16), mask)


def place_kernel(order_ref, *refs):
    out_ref = refs[-1]
    for k in range(N):
        first = pl.multiple_of(order_ref[k] * 2 * HD, 2 * HD)
        out_ref[:, pl.ds(first, 2 * HD)] = refs[k][...]


def placed(order, pieces):
    whole = lambda i, order: (0, 0)
    grid_spec = pltpu.PrefetchScalarGridSpec(
        num_scalar_prefetch=1,
        grid=(1,),
        in_specs=[pl.BlockSpec((R_TOK, 2 * HD), whole)] * N,
        out_specs=pl.BlockSpec((R_TOK, QH * HD), whole),
    )
    return pl.pallas_call(
        place_kernel,
        grid_spec=grid_spec,
        out_shape=jax.ShapeDtypeStruct((R_TOK, QH * HD), bf16),
        name="placed",
    )(order, *pieces)


def per_device(
    patches,
    vis_gain,
    w_qkv,
    w_out,
    merge_gain,
    w_merge,
    token_dest,
    token_row,
    prompt_text,
    kv_gain,
    w_kv,
    queries,
    resp_kv,
    resp_len,
):
    ctx_index = lax.axis_index("ctx")
    vis_index = lax.axis_index("vis")
    group = vis_index // 4

    rows = jnp.arange(LOCAL + VHD, dtype=jnp.int32)
    source = jnp.where(rows < LOCAL, rows % 32 * 4 + rows // 32, -1)
    from_patches = (source[:, None] == jnp.arange(LOCAL, dtype=jnp.int32)[None, :]).astype(bf16)
    from_out = (rows[:, None] - LOCAL == jnp.arange(VHD, dtype=jnp.int32)[None, :]).astype(bf16)
    block = dot(from_patches, patches, (1, 0)) + dot(from_out, w_out, (1, 0))
    image = lax.all_gather(block.astype(bf16), "vis", axis=0)
    w_turned = jnp.transpose(w_qkv, (1, 0))

    w_kv_mine = w_kv.T.reshape(2, KVH, 2, 64, 512).transpose(1, 0, 2, 3, 4).reshape(1024, 512)
    text = prompt_text.astype(f32)
    text_squares = jnp.sum(text * text, axis=1)
    text_gained = (text * kv_gain).astype(bf16)
    text_part = dot(w_kv_mine, text_gained, (1, 1)).reshape(N, 64, CROWS)
    text_extra = jnp.broadcast_to(text_squares[None, None, :], (N, 8, CROWS))
    text_part = jnp.concatenate([text_part, text_extra], axis=1).reshape(N * CHUNK, CROWS)

    own_q = lax.dynamic_slice_in_dim(queries, vis_index * 256, 256, 1)
    vis_row = vis_gain.reshape(1, VD)
    own_q, text_part, vis_row = lax.optimization_barrier((own_q, text_part, vis_row))
    half = R_TOK // 2
    qa = lax.all_gather(own_q[:half], "ctx", axis=0)
    qb = lax.all_gather(own_q[half:], "ctx", axis=0)

    flat_dest = token_dest.reshape(-1)
    flat_row = token_row.reshape(-1)
    here = jnp.where(flat_dest == ctx_index, flat_row // 128, -1)
    tall = (here[None, :] == jnp.arange(8, dtype=jnp.int32)[:, None]).astype(bf16)
    wide = ((flat_row % 128)[:, None] == jnp.arange(128, dtype=jnp.int32)[None, :]).astype(bf16)
    taken = dot(tall, wide, (1, 0)).reshape(1, CROWS)
    mask = jnp.where(taken > 0.5, NEG, 0.0)
    mask = jnp.concatenate([mask, jnp.zeros((1, VTOK), f32)], axis=1)

    own_k = lax.dynamic_slice_in_dim(resp_kv, group * HD, HD, 1)
    own_v = lax.dynamic_slice_in_dim(resp_kv, KVH * HD + group * HD, HD, 1)
    positions = jnp.arange(R_TOK, dtype=jnp.int32)
    visible = positions[None, :] <= positions[:, None]
    q_two = own_q.reshape(R_TOK, 2, HD)
    own_scores = jnp.einsum("rhd,nd->hrn", q_two, own_k, preferred_element_type=f32)
    own_scores = jnp.where(visible, own_scores * (1.0 / math.sqrt(HD)), NEG)
    own_high = jnp.max(own_scores, axis=2, keepdims=True)
    own_expo = jnp.where(visible, jnp.exp(own_scores - own_high), 0.0)
    own_total = jnp.sum(own_expo, axis=2, keepdims=True)
    own_mixed = jnp.einsum("hrn,nd->hrd", own_expo.astype(bf16), own_v, preferred_element_type=f32)
    own_mixed = (own_mixed / own_total).reshape(256, HD)
    own_level = (own_high * LOG2E + jnp.log2(own_total)).reshape(1, 256)

    image, qa, qb, text_part = lax.optimization_barrier((image, qa, qb, text_part))
    own_heads = vision(image, vis_row, w_turned)
    text_sum = lax.psum_scatter(text_part, "vis", scatter_dimension=0, tiled=True)
    text_scale = lax.rsqrt(text_sum[64:65] / D + EPS)
    text_kv = (text_sum[:64] * text_scale).astype(bf16)
    owners = ring_owners(vis_index)
    partial = merge(
        owners,
        ring_gather(own_heads),
        image,
        merge_gain.reshape(1, VD),
        w_merge,
        kv_gain.reshape(1, 512),
        w_kv_mine,
    )
    arrived = lax.all_to_all(partial, "vis", split_axis=0, concat_axis=0, tiled=True)
    arrived, text_kv = lax.optimization_barrier((arrived, text_kv))
    vis_sum = jnp.sum(arrived.astype(f32), axis=0)
    vis_squares = vis_sum[64:65] + vis_sum[65:66] + vis_sum[66:67]
    vis_kv = (vis_sum[:64] * lax.rsqrt(vis_squares / D + EPS)).astype(bf16)
    kv = jnp.concatenate([text_kv, vis_kv], axis=1)
    kv = lax.all_gather(kv, "vis", axis=0, tiled=True, axis_index_groups=QUADS)
    packed = response(qa, qb, kv, mask)
    back = lax.all_to_all(packed, "ctx", split_axis=0, concat_axis=0, tiled=True).astype(f32)
    levels = back[:, 256:258] + back[:, 258:260] + back[:, 260:262]
    levels = levels.reshape(N, 256)
    highest = jnp.maximum(jnp.max(levels, axis=0, keepdims=True), own_level)
    weights = jnp.exp2(levels - highest)
    own_weight = jnp.exp2(own_level - highest)
    total = jnp.sum(weights, axis=0, keepdims=True) + own_weight
    weights = weights / total
    own_weight = own_weight / total
    result = jnp.sum(back[:, :256] * weights[:, :, None], axis=0)
    result = result + own_mixed * own_weight.reshape(256, 1)
    result = jnp.transpose(result.reshape(2, R_TOK, HD), (1, 0, 2)).reshape(R_TOK, 256)
    live = (positions < resp_len[0])[:, None]
    result = jnp.where(live, result, 0.0).astype(bf16)
    return placed(owners, short_gather(result))


def solution(mesh):
    return jax.shard_map(
        per_device,
        mesh=mesh,
        in_specs=(
            P(("ctx", "vis"), None),
            P(),
            P(None, "vis"),
            P("vis", None),
            P(),
            P(None, "vis"),
            P(),
            P(),
            P("ctx", "vis"),
            P("vis"),
            P("vis", None),
            P("ctx", None),
            P("ctx", None),
            P("ctx"),
        ),
        out_specs=P("ctx", None),
        check_vma=False,
    )
```
